128 devices in a mesh: wave: 64 (over z, y, x), lev: 2 (over core).
Axes of the slice: x: 4, y: 4, z: 4, core: 2. Of those that a mesh axis runs over, the one named last changes fastest.
Arguments:
- spectral_state: bfloat16 [4, 128, 819840], P(None, 'lev', 'wave'), may hold values from -6 to 6
- legendre_basis: bfloat16 [819840, 128], P('wave'), may hold values from -0.15625 to 0.15625
- pairing: int32 [64, 10], replicated, may hold values from 0 to 63, as said below
- band_rows: int32 [64], replicated, may hold values from 1 to 4, 128 in all
- weights: float32 [128], replicated, may hold values from 1 to 6
- mode_rates: float32 [128], replicated, may hold values from 0.05 to 20
Outputs:
- new_state: bfloat16 [4, 128, 819840], P(None, 'lev', 'wave')
- band_terms: bfloat16 [256, 2, 128, 2688], P('wave', None, 'lev')
The draws below stay inside these ranges and needn't reach their ends.
Inputs may be any that keep to these rules, and one draw needn't show every extreme that they name: `pairing`: each column is a permutation of the 64 devices' numbers 0 to 63. `band_rows`: the entries sum to 128.
All inputs are finite; a program needn't handle non-finite values.
Results may differ from the reference program's by a relative error of at most 0.0095.
Values may be sent and summed in bfloat16 or wider, within the bound.
A program may use at most 192 MiB of HBM per device.

```python
import math
import jax
import jax.numpy as jnp
import numpy as np
from jax import lax

M = 1280
NLON = 2688
LEV = 128
CAP = 4
LAT = 128
PAIRS_DEV = 12810
ROWS = 819840
N_WAVE = 64


def draw_pairing(key, part):
    key = jax.random.fold_in(key, 11)
    round_keys = jax.random.split(key, M // (2 * N_WAVE))
    columns = jax.vmap(lambda round_key: jax.random.permutation(round_key, N_WAVE))(round_keys)
    return columns.T.astype(jnp.int32)


def levels(own_key, dims, cuts, smallest, top_value):
    factor_of = 1.0
    for position, shards_of in cuts:
        heights = jax.random.uniform(jax.random.fold_in(jax.random.fold_in(own_key, 6), position), (shards_of,), jnp.float32, smallest / len(cuts), top_value / len(cuts))
        factor_of = factor_of * jnp.repeat(jnp.exp(heights), dims[position] // shards_of).reshape((-1,) + (1,) * (len(dims) - 1 - position))
    return factor_of


def profile(number_of, total, bound, skew):
    weights = [(1 << 20) // math.isqrt(grade ** skew) + 1 for grade in range(2, number_of + 1)]
    surplus, holding = total - bound - (number_of - 1), [1] * (number_of - 1)
    while surplus > 0:
        candidates = [i for i in range(number_of - 1) if holding[i] < bound]
        mass, remaining = sum([weights[i] for i in candidates]), surplus
        for i in candidates:
            more = min(bound - holding[i], max(1, remaining * weights[i] // mass), surplus)
            holding[i] = holding[i] + more
            surplus = surplus - more
    return np.array([bound] + holding)


def uneven(key, amount, total, most, lean):
    if amount == 2:
        one = jax.random.randint(key, (), max(1, total - most), min(most, total - 1) + 1)
        return jnp.stack([one, total - one])
    lengths = jnp.asarray(profile(amount, total, most, lean), jnp.int32)
    twos = (amount - 1) // 2
    donor, taker = lengths[1:1 + 2 * twos:2], lengths[2:2 + 2 * twos:2]
    room = jnp.minimum(donor - 1, most - taker)
    moved = jax.random.randint(jax.random.fold_in(key, 1), (twos,), 0, 1 << 20) % (room + 1)
    lengths = lengths.at[1:1 + 2 * twos:2].set(donor - moved).at[2:2 + 2 * twos:2].set(taker + moved)
    return lengths[jax.random.permutation(jax.random.fold_in(key, 2), amount)]


def noise(own_key, extent, deviation, bound, cuts=(), kind=jnp.bfloat16):
    loudness = levels(own_key, extent, cuts, -0.22, 0.18) if cuts else 1.0
    entries = jax.random.normal(own_key, extent, jnp.float32) * deviation * loudness
    return jnp.minimum(jnp.maximum(entries, -bound), bound).astype(kind)


def setup_inputs(seed: int = 0) -> dict:
    key_of = jax.random.split(jax.random.key(seed), 7)
    spectral_state = noise(key_of[0], (4, LEV, ROWS), 1.0, 6.0, ((1, 2), (2, 64)))
    legendre_basis = noise(key_of[1], (ROWS, LAT), M ** -0.5, 0.15625, ((0, 64),))
    pairing = draw_pairing(jax.random.fold_in(key_of[6], 71), 0)
    band_rows = uneven(key_of[3], N_WAVE, LAT, CAP, 2).astype(jnp.int32)
    weights = jnp.clip(jnp.exp(jax.random.uniform(key_of[4], (LAT,), jnp.float32, math.log(1.0), math.log(6.0))), 1.0, 6.0)
    mode_rates = jnp.clip(jnp.exp(jax.random.uniform(key_of[5], (LEV,), jnp.float32, math.log(0.05), math.log(20.0))), 0.05, 20.0)
    return dict(spectral_state=spectral_state, legendre_basis=legendre_basis, pairing=pairing, band_rows=band_rows, weights=weights, mode_rates=mode_rates)


STEP_WEIGHT = 0.5
IMPLICIT_WEIGHT = 1.0

def piece_table(pair_row, wave_count):
    layout = []
    offset = 0
    for piece_index in range(M // (2 * wave_count)):
        length = 2 * M - 4 * piece_index * wave_count - 2 * wave_count + 1
        lower_wave = 2 * piece_index * wave_count + pair_row[piece_index]
        upper_wave = 2 * piece_index * wave_count + 2 * wave_count - 1 - pair_row[piece_index]
        layout.append((offset, length, lower_wave, upper_wave, M - lower_wave))
        offset += length
    return layout

def wave_numbers(pairing, wave_count):
    piece_base = 2 * wave_count * jnp.arange(M // (2 * wave_count), dtype=jnp.int32)
    lower_wave = piece_base[None, :] + pairing
    upper_wave = piece_base[None, :] + 2 * wave_count - 1 - pairing
    return jnp.stack([lower_wave, upper_wave], axis=2).reshape(pairing.shape[0], -1).astype(jnp.int32)

def wave_tables(wave_ids, lon_count):
    longitude = jnp.arange(lon_count, dtype=jnp.int32)
    phase_turns = wave_ids[:, None] * longitude[None, :] % lon_count
    angles = 2.0 * math.pi / lon_count * phase_turns.astype(jnp.float32)
    scaling = lon_count ** (-0.5)
    weighting = jnp.where(wave_ids == 0, 1.0, 2.0)[:, None] * scaling
    cosines = jnp.cos(angles)
    sine_part = jnp.sin(angles)
    synthesis = jnp.stack([weighting * cosines, -weighting * sine_part], axis=1).astype(jnp.bfloat16)
    analysis = jnp.stack([scaling * cosines, -scaling * sine_part], axis=1).astype(jnp.bfloat16)
    return (synthesis, analysis)

def vertical_modes(count):
    level_ids = jnp.arange(count, dtype=jnp.float32)
    mode_vectors = math.sqrt(2.0 / count) * jnp.cos(math.pi * (level_ids[:, None] + 0.5) * level_ids[None, :] / count)
    return jnp.where(level_ids[None, :] == 0.0, mode_vectors * math.sqrt(0.5), mode_vectors)

def implicit_factor(degree, mode_rates):
    degree_real = degree.astype(jnp.float32)
    spread = degree_real * (degree_real + 1.0) / float(M * M)
    return 1.0 / (1.0 + IMPLICIT_WEIGHT * mode_rates[:, None] * spread[None, :])

def inverse_device(basis_dev, flat_dev, pair_row):
    products = []
    degrees = []
    for offset, length, lower_wave, upper_wave, split_row in piece_table(pair_row, N_WAVE):
        row_ids = jnp.arange(length, dtype=jnp.int32)
        in_lower = row_ids < split_row
        state_block = flat_dev[:, offset:offset + length]
        zeros_block = jnp.zeros_like(state_block)
        masked_pair = jnp.concatenate([jnp.where(in_lower[None, :], state_block, zeros_block), jnp.where(in_lower[None, :], zeros_block, state_block)], axis=0)
        products.append(jnp.dot(basis_dev[offset:offset + length].T, masked_pair.T, preferred_element_type=jnp.float32))
        degrees.append(jnp.where(in_lower, lower_wave + row_ids, upper_wave + row_ids - split_row).astype(jnp.int32))
    return (jnp.concatenate(products, axis=1), jnp.concatenate(degrees))

def direct_device(basis_dev, weighted_dev, pair_row, comps):
    products = []
    for piece_index, (offset, length, lower_wave, upper_wave, split_row) in enumerate(piece_table(pair_row, N_WAVE)):
        row_ids = jnp.arange(length, dtype=jnp.int32)
        in_lower = row_ids < split_row
        columns = weighted_dev[:, 2 * piece_index * comps:(2 * piece_index + 2) * comps]
        paired = jnp.dot(columns.T, basis_dev[offset:offset + length].T, preferred_element_type=jnp.float32)
        products.append(jnp.where(in_lower[None, :], paired[:comps], paired[comps:]))
    return jnp.concatenate(products, axis=1)

def couple(blended_state, degree, mode_rates):
    mode_vectors = vertical_modes(LEV)
    damping_factor = implicit_factor(degree, mode_rates)
    projected_state = jnp.einsum('ba,sbw->saw', mode_vectors, blended_state.astype(jnp.float32), precision=lax.Precision.HIGHEST)
    return jnp.einsum('xn,tng->txg', mode_vectors, projected_state * damping_factor[None], precision=lax.Precision.HIGHEST)

def reference(spectral_state, legendre_basis, pairing, band_rows, weights, mode_rates):
    comps = 4 * LEV
    m_local = M // N_WAVE
    flat_state = spectral_state.reshape(comps, N_WAVE, PAIRS_DEV).transpose(1, 0, 2)
    basis_blocks = legendre_basis.reshape(N_WAVE, PAIRS_DEV, LAT)

    def forward(carry, input_fields):
        basis_dev, flat_dev, pair_row = input_fields
        coefficients, degree = inverse_device(basis_dev, flat_dev, pair_row)
        return (carry, (coefficients.astype(jnp.bfloat16), degree))
    _, (fourier, degree) = lax.scan(forward, None, (basis_blocks, flat_state, pairing))
    fourier = fourier.reshape(N_WAVE, LAT, m_local, 2, 2, LEV)
    synthesis, analysis = wave_tables(wave_numbers(pairing, N_WAVE).reshape(-1), NLON)
    synthesis = synthesis.reshape(N_WAVE, m_local, 2, NLON)
    analysis = analysis.reshape(N_WAVE, m_local, 2, NLON)
    grid_values = jnp.einsum('eaifrl,eirn->afln', fourier.astype(jnp.float32), synthesis.astype(jnp.float32), precision=lax.Precision.HIGHEST)
    u_grid = grid_values[:, 0]
    v_grid = grid_values[:, 1]
    grid_terms = jnp.stack([-u_grid * v_grid, 0.5 * (u_grid * u_grid - v_grid * v_grid)], axis=1).astype(jnp.bfloat16)
    coefficients = jnp.einsum('afln,eirn->eaifrl', grid_terms.astype(jnp.float32), analysis.astype(jnp.float32), precision=lax.Precision.HIGHEST).astype(jnp.bfloat16)
    weighted = (weights[None, :, None, None, None, None] * coefficients.astype(jnp.float32)).astype(jnp.bfloat16)
    weighted = weighted.reshape(N_WAVE, LAT, m_local * comps)
    state_blocks = spectral_state.reshape(4, LEV, N_WAVE, PAIRS_DEV).transpose(2, 0, 1, 3)

    def backward(carry, input_fields):
        basis_dev, weighted_dev, pair_row, state_dev, degree_dev = input_fields
        tendency = direct_device(basis_dev, weighted_dev, pair_row, comps).reshape(4, LEV, PAIRS_DEV)
        blended_state = (state_dev.astype(jnp.float32) + STEP_WEIGHT * tendency).astype(jnp.bfloat16)
        return (carry, couple(blended_state, degree_dev, mode_rates).astype(jnp.bfloat16))
    _, updated = lax.scan(backward, None, (basis_blocks, weighted, pairing, state_blocks, degree))
    new_state = updated.transpose(1, 2, 0, 3).reshape(4, LEV, ROWS)
    starts = (jnp.cumsum(band_rows) - band_rows).astype(jnp.int32)
    slot_ids = jnp.arange(CAP, dtype=jnp.int32)
    lat_index = jnp.clip(starts[:, None] + slot_ids[None, :], 0, LAT - 1).astype(jnp.int32)
    interior_terms = (slot_ids[None, :] < band_rows[:, None]).reshape(-1)
    picked = grid_terms[lat_index.reshape(-1)]
    band_terms = jnp.where(interior_terms[:, None, None, None], picked, jnp.zeros_like(picked))
    return (new_state, band_terms)
```

```python
import functools
import math

import jax
import jax.numpy as jnp
from jax import lax
from jax.experimental import pallas as pl
from jax.experimental.pallas import tpu as pltpu
from jax.sharding import PartitionSpec as P

M = 1280
NLON = 2688
HALF = NLON // 2
HPAD = 1408
LAT = 128
NW = 64
NR = 12810
LEV = 128
LEVD = 64
ROUNDS = M // (2 * NW)
CHUNKS = ROUNDS // 2
PIECES = []
_offset = 0
for _k in range(ROUNDS):
    _length = 2 * M - 4 * _k * NW - 2 * NW + 1
    PIECES.append((_offset, _length))
    _offset += _length
WINDOWS = [(o // 128 * 128, min(-(-(o + n) // 128) * 128, NR)) for o, n in PIECES]
STEP_WEIGHT = 0.5
VMEM_LIMIT = 60 * 1024 * 1024
BF = jnp.bfloat16
F32 = jnp.float32
NN = (((1,), (0,)), ((), ()))
NT = (((1,), (1,)), ((), ()))
TN = (((0,), (0,)), ((), ()))
TT = (((0,), (1,)), ((), ()))


def mm(a, b, dims):
    return lax.dot_general(a, b, dims, preferred_element_type=F32)


def masked_basis(basis_ref, ranges_ref, k):
    a, b = WINDOWS[k]
    rows = a + lax.broadcasted_iota(jnp.int32, (b - a, 1), 0)
    block = basis_ref[a:b, :].astype(F32)
    even = (rows >= ranges_ref[0, k]) & (rows < ranges_ref[1, k])
    odd = (rows >= ranges_ref[2, k]) & (rows < ranges_ref[3, k])
    return jnp.concatenate(
        [jnp.where(even, block, 0.0).astype(BF), jnp.where(odd, block, 0.0).astype(BF)], axis=1
    )


def inverse_kernel(ranges_ref, scale_ref, state_ref, basis_ref, pick_ref, home_ref, extra_ref, sa, sb):
    for ch in range(CHUNKS):
        for kk in range(2):
            k = 2 * ch + kk
            a, b = WINDOWS[k]
            both = masked_basis(basis_ref, ranges_ref, k)
            rows = jnp.concatenate([state_ref[c, :, a:b] for c in (0, 2, 1, 3)], axis=0)
            product = mm(rows, both, NN)
            for par in range(2):
                part = product[:, par * LAT : (par + 1) * LAT]
                if k == 0 and par == 0:
                    part = part * scale_ref[0]
                picked = mm(pick_ref[...], part.astype(BF), NT)
                for r in range(2):
                    for slot in range(2):
                        at = kk * 8 + r * 4 + slot * 2 + par
                        lanes = slice(r * 128, (r + 1) * 128)
                        sa[pl.ds(at, NW, stride=16), :] = picked[slot * NW : (slot + 1) * NW, lanes]
                        sb[pl.ds(at, NW, stride=16), :] = picked[(2 + slot) * NW : (3 + slot) * NW, lanes]
        home_ref[:, ch * 16 : (ch + 1) * 16, :] = sa[...].reshape(NW, 16, 128).astype(BF)
        extra_ref[:, ch * 16 : (ch + 1) * 16, :] = sb[...].reshape(NW, 16, 128).astype(BF)


def synthesize(x_ref, table_ref, sx, acc):
    for ch in range(CHUNKS):
        sx[...] = x_ref[:, ch * 16 : (ch + 1) * 16, :].astype(F32).reshape(NW * 16, 128)
        for par in range(2):
            spectra = jnp.concatenate(
                [sx[pl.ds(slot * 2 + par, 256, stride=4), :] for slot in range(2)], axis=1
            ).astype(BF)
            part = mm(spectra, table_ref[par, ch], TN)
            if ch == 0:
                acc[par] = part
            else:
                acc[par] = acc[par] + part


def slot_terms(acc, slot):
    base = slot * 128
    eu, ev = acc[0, base : base + 64, :], acc[0, base + 64 : base + 128, :]
    ou, ov = acc[1, base : base + 64, :], acc[1, base + 64 : base + 128, :]
    out = []
    for u, v in ((eu + ou, ev + ov), (eu - ou, ev - ov)):
        out.append(((-4.0 * u * v).astype(BF), (2.0 * (u * u - v * v)).astype(BF)))
    return out


def grid_kernel(w_ref, x_ref, table_ref, terms_ref, coeff_ref, sx, acc, tp):
    synthesize(x_ref, table_ref, sx, acc)
    for slot in range(2):
        first, second = slot_terms(acc, slot)
        for f in range(2):
            at = slot * 128 + f * 64
            terms_ref[0, at : at + 64, :] = first[f]
            terms_ref[1, at : at + 64, :] = second[f]
            p, q = first[f].astype(F32), second[f].astype(F32)
            tp[0, at : at + 64, :] = (p + q).astype(BF)
            tp[1, at : at + 64, :] = (p - q).astype(BF)
    for ch in range(CHUNKS):
        for par in range(2):
            coeff = mm(table_ref[par, ch], tp[par], NT).astype(BF).astype(F32)
            for slot in range(2):
                sx[pl.ds(slot * 2 + par, 256, stride=4), :] = (
                    coeff[:, slot * 128 : (slot + 1) * 128] * w_ref[slot]
                )
        coeff_ref[:, ch * 16 : (ch + 1) * 16, :] = sx[...].reshape(NW, 16, 128).astype(BF)


def store_band(out_ref, slot, f, first, second, keep):
    p = jnp.where(keep, first.astype(F32), 0.0)
    q = jnp.where(keep, second.astype(F32), 0.0)
    rolled = pltpu.roll(q, 64, axis=1)
    out_ref[slot, f, :, 0:1280] = p[:, 0:1280].astype(BF)
    out_ref[slot, f, :, 1280:1408] = (p[:, 1280:1408] + rolled[:, 0:128]).astype(BF)
    out_ref[slot, f, :, 1408:2688] = rolled[:, 128:1408].astype(BF)


def band_kernel(rows_ref, terms_ref, x_ref, table_ref, out_ref, sx, acc):
    synthesize(x_ref, table_ref, sx, acc)
    for slot in range(2):
        first, second = slot_terms(acc, slot)
        for f in range(2):
            at = slot * 128 + f * 64
            store_band(
                out_ref, slot, f, terms_ref[0, at : at + 64, :], terms_ref[1, at : at + 64, :], rows_ref[0] > slot
            )
            store_band(out_ref, 2 + slot, f, first[f], second[f], rows_ref[0] > 2 + slot)


def coupled_kernel(spread_ref, rates_ref, own_ref, other_ref, down_ref, up_ref, out_ref):
    tile = 1408
    for a in range(0, NR, tile):
        b = min(a + tile, NR)
        factor = 1.0 / (1.0 + rates_ref[...] * spread_ref[0:1, a:b])
        factor = jnp.concatenate([factor, factor], axis=0)
        for r in range(2):
            levels = jnp.concatenate(
                [own_ref[r, :, a:b], own_ref[2 + r, :, a:b], other_ref[r, :, a:b], other_ref[2 + r, :, a:b]],
                axis=0,
            )
            modes = (mm(down_ref[...], levels, NN) * factor).astype(BF)
            result = mm(up_ref[...], modes, NN).astype(BF)
            out_ref[r, :, a:b] = result[0:64]
            out_ref[2 + r, :, a:b] = result[64:128]


def direct_kernel(
    ranges_ref, spread_ref, rates_ref, basis_ref, own_ref, other_ref, unpick_ref, down_ref, up_ref, base_ref, out_ref, so, sp
):
    out_ref[...] = base_ref[...]
    for ch in range(CHUNKS):
        so[...] = own_ref[:, ch * 16 : (ch + 1) * 16, :].astype(F32).reshape(NW * 16, 128)
        sp[...] = other_ref[:, ch * 16 : (ch + 1) * 16, :].astype(F32).reshape(NW * 16, 128)
        for kk in range(2):
            k = 2 * ch + kk
            a, b = WINDOWS[k]
            both = masked_basis(basis_ref, ranges_ref, k)
            factor = STEP_WEIGHT / (1.0 + rates_ref[...] * spread_ref[0:1, a:b])
            factor = jnp.concatenate([factor, factor], axis=0)
            for r in range(2):
                weighted = []
                for par in range(2):
                    at = [kk * 8 + r * 4 + slot * 2 + par for slot in range(2)]
                    gathered = jnp.concatenate(
                        [
                            jnp.concatenate([s[pl.ds(i, NW, stride=16), :] for i in at], axis=0)
                            for s in (so, sp)
                        ],
                        axis=1,
                    ).astype(BF)
                    by_lat = mm(unpick_ref[...], gathered, NN).astype(BF)
                    weighted.append(mm(by_lat, down_ref[...], NT).astype(BF))
                pair = jnp.concatenate(weighted, axis=0)
                modes = (mm(pair, both, TT) * factor).astype(BF)
                change = mm(up_ref[...], modes, NN)
                for f in range(2):
                    c = 2 * f + r
                    out_ref[c, :, a:b] = (
                        out_ref[c, :, a:b].astype(F32) + change[f * 64 : (f + 1) * 64]
                    ).astype(BF)


def vertical_modes():
    ids = jnp.arange(LEV, dtype=F32)
    vectors = math.sqrt(2.0 / LEV) * jnp.cos(math.pi * (ids[:, None] + 0.5) * ids[None, :] / LEV)
    return jnp.where(ids[None, :] == 0.0, vectors * math.sqrt(0.5), vectors)


def cos_table(waves):
    lon = lax.broadcasted_iota(jnp.int32, (1, 1, 1, 1, 1, HPAD), 5).astype(F32)
    part = lax.broadcasted_iota(jnp.int32, (1, 1, 1, 1, 2, 1), 4).astype(F32)
    turns = waves.astype(F32)[..., None, None] * lon + part * float(NLON // 4)
    rest = turns - jnp.floor(turns * (1.0 / NLON) + 0.5) * float(NLON)
    y = rest * (math.pi / NLON)
    z = y * y
    series = -1.0 / 39916800.0
    for term in (1.0 / 362880.0, -1.0 / 5040.0, 1.0 / 120.0, -1.0 / 6.0, 1.0):
        series = series * z + term
    half_sine = y * series
    cosine = (1.0 - 2.0 * half_sine * half_sine) * (NLON ** -0.5)
    return jnp.where(lon < HALF, cosine, 0.0).astype(BF).reshape(2, CHUNKS, 4 * NW, HPAD)


def call(kernel, out_shape, scratch, operands, smem, flops, nbytes, aliases=None):
    vmem = pl.BlockSpec(memory_space=pltpu.VMEM)
    return pl.pallas_call(
        kernel,
        out_shape=out_shape,
        in_specs=[pl.BlockSpec(memory_space=pltpu.SMEM)] * smem + [vmem] * (len(operands) - smem),
        out_specs=jax.tree.map(lambda _: vmem, out_shape),
        scratch_shapes=scratch,
        compiler_params=pltpu.CompilerParams(vmem_limit_bytes=VMEM_LIMIT),
        cost_estimate=pl.CostEstimate(flops=flops, bytes_accessed=nbytes, transcendentals=0),
        input_output_aliases=aliases or {},
    )(*operands)


def local(spectral_state, legendre_basis, pairing, band_rows, weights, mode_rates):
    wave = lax.axis_index("wave")
    lev = lax.axis_index("lev")
    other_state = lax.ppermute(spectral_state, "lev", [(0, 1), (1, 0)])
    pair = lax.dynamic_index_in_dim(pairing, wave, 0, keepdims=False)
    rounds = jnp.arange(ROUNDS, dtype=jnp.int32)
    low = 2 * NW * rounds + pair
    high = 2 * NW * rounds + 2 * NW - 1 - pair
    begin = jnp.asarray([o for o, _ in PIECES], jnp.int32)
    end = jnp.asarray([o + n for o, n in PIECES], jnp.int32)
    split = begin + M - low
    low_even = low % 2 == 0
    ranges = jnp.stack(
        [
            jnp.where(low_even, begin, split),
            jnp.where(low_even, split, end),
            jnp.where(low_even, split, begin),
            jnp.where(low_even, end, split),
        ]
    )
    degree = jnp.concatenate(
        [
            jnp.where(
                jnp.arange(n) < M - low[k],
                low[k] + jnp.arange(n, dtype=jnp.int32),
                high[k] - (M - low[k]) + jnp.arange(n, dtype=jnp.int32),
            )
            for k, (_, n) in enumerate(PIECES)
        ]
    ).astype(F32)
    spread = (degree * (degree + 1.0) / float(M * M))[None, :]
    rates = mode_rates[:, None]
    zero_scale = jnp.where(low[0:1] == 0, 0.5, 1.0).astype(F32)

    starts = jnp.cumsum(band_rows) - band_rows
    single = band_rows == 1
    lat_ids = jnp.arange(LAT, dtype=jnp.int32)
    owner_hit = (starts[None, :] <= lat_ids[:, None]) & (lat_ids[:, None] < (starts + band_rows)[None, :])
    slot_of = jnp.sum(jnp.where(owner_hit, lat_ids[:, None] - starts[None, :], 0), axis=1)
    is_extra = slot_of >= 2
    extra_rank = jnp.cumsum(is_extra.astype(jnp.int32)) - 1
    single_rank = jnp.cumsum(single.astype(jnp.int32)) - 1
    adopted = jnp.sum(
        jnp.where(is_extra[None, :] & (extra_rank[None, :] == single_rank[:, None]), lat_ids[None, :], 0), axis=1
    )
    home_second = jnp.where(single, adopted, starts + 1)
    slots = jnp.concatenate(
        [starts, home_second, jnp.minimum(starts + 2, LAT - 1), jnp.minimum(starts + 3, LAT - 1)]
    )
    pick_bool = slots[:, None] == lat_ids[None, :]
    pick = pick_bool.astype(BF)
    unpick = pick[: 2 * NW].T
    slot_weights = jnp.sum(jnp.where(pick_bool[: 2 * NW], weights[None, :], 0.0), axis=1)
    own_weights = jnp.stack([slot_weights[wave], slot_weights[NW + wave]])
    own_rows = band_rows[wave][None]

    modes = vertical_modes()
    mine = lax.dynamic_slice_in_dim(modes, lev * LEVD, LEVD, 0)
    theirs = lax.dynamic_slice_in_dim(modes, (1 - lev) * LEVD, LEVD, 0)
    none = jnp.zeros((LEVD, LEV), F32)
    up = jnp.concatenate(
        [jnp.concatenate([mine, none], axis=1), jnp.concatenate([none, mine], axis=1)], axis=0
    ).astype(BF)
    up_other = jnp.concatenate(
        [jnp.concatenate([theirs, none], axis=1), jnp.concatenate([none, theirs], axis=1)], axis=0
    ).astype(BF)
    down = jnp.concatenate([up, up_other], axis=0).T

    message = jax.ShapeDtypeStruct((NW, 16 * CHUNKS, 128), BF)
    chunk_scratch = pltpu.VMEM((NW * 16, 128), F32)
    home, extra = call(
        inverse_kernel,
        (message, message),
        [chunk_scratch, chunk_scratch],
        (ranges, zero_scale, spectral_state, legendre_basis, pick),
        2,
        2_000_000_000,
        13_000_000,
    )
    home_in = lax.all_to_all(home, "wave", split_axis=0, concat_axis=0, tiled=True)

    all_low = 2 * NW * rounds[None, :] + pairing
    all_high = 2 * NW * rounds[None, :] + 2 * NW - 1 - pairing
    all_even = all_low % 2 == 0
    waves = jnp.stack([jnp.where(all_even, all_low, all_high), jnp.where(all_even, all_high, all_low)])
    waves = waves.reshape(2, NW, CHUNKS, 2).transpose(0, 2, 1, 3)
    table = cos_table(waves)

    base = call(
        coupled_kernel,
        jax.ShapeDtypeStruct((4, LEVD, NR), BF),
        [],
        (spread, rates, spectral_state, other_state, down, up),
        0,
        10_000_000_000,
        20_000_000,
    )

    acc = pltpu.VMEM((2, 256, HPAD), F32)
    terms, coeff = call(
        grid_kernel,
        (jax.ShapeDtypeStruct((2, 256, HPAD), BF), message),
        [chunk_scratch, acc, pltpu.VMEM((2, 256, HPAD), BF)],
        (own_weights, home_in, table),
        1,
        3_600_000_000,
        12_000_000,
    )
    coeff_in = lax.all_to_all(coeff, "wave", split_axis=0, concat_axis=0, tiled=True)
    extra_in = lax.all_to_all(extra, "wave", split_axis=0, concat_axis=0, tiled=True)
    coeff_other = lax.ppermute(coeff_in, "lev", [(0, 1), (1, 0)])
    band_terms = call(
        band_kernel,
        jax.ShapeDtypeStruct((4, 2, LEVD, NLON), BF),
        [chunk_scratch, acc],
        (own_rows, terms, extra_in, table),
        1,
        1_800_000_000,
        13_000_000,
    )
    new_state = call(
        direct_kernel,
        jax.ShapeDtypeStruct((4, LEVD, NR), BF),
        [chunk_scratch, chunk_scratch],
        (ranges, spread, rates, legendre_basis, coeff_in, coeff_other, unpick, down, up, base),
        1,
        6_000_000_000,
        20_000_000,
        None,
    )
    return (new_state, band_terms)


def solution(mesh):
    in_specs = (P(None, "lev", "wave"), P("wave", None), P(), P(), P(), P())
    out_specs = (P(None, "lev", "wave"), P("wave", None, "lev", None))
    return jax.shard_map(local, mesh=mesh, in_specs=in_specs, out_specs=out_specs, check_vma=False)
```

```python
import math

import jax
import jax.numpy as jnp
from jax import lax
from jax.experimental import pallas as pl
from jax.experimental.pallas import tpu as pltpu
from jax.sharding import PartitionSpec as P

M = 1280
NLON = 2688
HALF = NLON // 2
TILES = 11
HPAD = 128 * TILES
LAT = 128
NW = 64
NR = 12810
LEV = 128
LEVD = 64
ROUNDS = M // (2 * NW)
CHUNKS = ROUNDS // 2
PIECES = []
_offset = 0
for _k in range(ROUNDS):
    _length = 2 * M - 4 * _k * NW - 2 * NW + 1
    PIECES.append((_offset, _length))
    _offset += _length
WINDOWS = [(o // 128 * 128, min(-(-(o + n) // 128) * 128, NR)) for o, n in PIECES]
STEP_WEIGHT = 0.5
VMEM_LIMIT = 61 * 1024 * 1024
BF = jnp.bfloat16
F32 = jnp.float32
I32 = jnp.int32
MESH = pl.DeviceIdType.MESH
NN = (((1,), (0,)), ((), ()))
NT = (((1,), (1,)), ((), ()))
TN = (((0,), (0,)), ((), ()))
TT = (((0,), (1,)), ((), ()))


def mm(a, b, dims):
    return lax.dot_general(a, b, dims, preferred_element_type=F32)


def iota(shape, dim):
    return lax.broadcasted_iota(I32, shape, dim)


def cos_sin(turns, period):
    rest = turns - jnp.floor(turns * (1.0 / period) + 0.5) * float(period)
    y = rest * (math.pi / period)
    z = y * y
    s = -1.0 / 39916800.0
    for term in (1.0 / 362880.0, -1.0 / 5040.0, 1.0 / 120.0, -1.0 / 6.0, 1.0):
        s = s * z + term
    s = s * y
    c = 1.0 / 479001600.0
    for term in (-1.0 / 3628800.0, 1.0 / 40320.0, -1.0 / 720.0, 1.0 / 24.0, -0.5, 1.0):
        c = c * z + term
    return 1.0 - 2.0 * s * s, 2.0 * s * c


def round_scalars(pair_s, me, k):
    pair = pair_s[me, k]
    begin, length = PIECES[k]
    low = 2 * NW * k + pair
    high = 2 * NW * k + 2 * NW - 1 - pair
    split = begin + M - low
    even = lax.rem(pair, 2) == 0
    end = begin + length
    ranges = (
        jnp.where(even, begin, split),
        jnp.where(even, split, end),
        jnp.where(even, split, begin),
        jnp.where(even, end, split),
    )
    return low, high, split, ranges


def masked_basis(basis, ranges, k):
    a, b = WINDOWS[k]
    rows = a + iota((b - a, 1), 0)
    block = basis[a:b, :].astype(F32)
    even = (rows >= ranges[0]) & (rows < ranges[1])
    odd = (rows >= ranges[2]) & (rows < ranges[3])
    return jnp.concatenate(
        [jnp.where(even, block, 0.0).astype(BF), jnp.where(odd, block, 0.0).astype(BF)], axis=1
    )


def make_picks(rows_v, pick):
    d = iota((NW, NW), 0)
    e = iota((NW, NW), 1)
    count_row = rows_v[...]
    before = e < d
    count = jnp.sum(jnp.where(e == d, count_row, 0).astype(F32), axis=1, keepdims=True)
    starts = jnp.sum(jnp.where(before, count_row, 0).astype(F32), axis=1, keepdims=True)
    single_rank = jnp.sum(jnp.where(before & (count_row == 1), 1.0, 0.0), axis=1, keepdims=True)
    lat = iota((NW, LAT), 1).astype(F32)
    hit = (starts <= lat) & (lat < starts + count)
    slot = jnp.sum(jnp.where(hit, lat - starts, 0.0), axis=0, keepdims=True)
    extra = jnp.where(slot >= 1.5, 1.0, 0.0)
    ahead = jnp.where(iota((LAT, LAT), 0) < iota((LAT, LAT), 1), 1.0, 0.0).astype(BF)
    extra8 = jnp.broadcast_to(extra, (16, LAT)).astype(BF)
    rank = mm(extra8, ahead, NN)[0:1, :]
    adopted = (extra > 0.5) & (rank == single_rank)
    second = jnp.where(count < 1.5, jnp.where(adopted, 1.0, 0.0), jnp.where(lat == starts + 1.0, 1.0, 0.0))
    pick[0:NW, :] = jnp.where(lat == starts, 1.0, 0.0).astype(BF)
    pick[NW : 2 * NW, :] = second.astype(BF)
    pick[2 * NW : 3 * NW, :] = jnp.where(lat == starts + 2.0, 1.0, 0.0).astype(BF)
    pick[3 * NW : 4 * NW, :] = jnp.where(lat == starts + 3.0, 1.0, 0.0).astype(BF)


def make_modes(lev, up, down):
    def fill(mode_index, level_index, same):
        phase = ((2 * level_index + 1) * mode_index).astype(F32)
        cosine, _ = cos_sin(phase, 4 * LEV)
        scale = jnp.where(mode_index == 0, math.sqrt(1.0 / LEV), math.sqrt(2.0 / LEV))
        return jnp.where(same, cosine * scale, 0.0).astype(BF)

    i, j = iota((128, 256), 0), iota((128, 256), 1)
    up[...] = fill(j % LEV, lev * LEVD + i % LEVD, i // LEVD == j // LEV)
    i, j = iota((256, 256), 0), iota((256, 256), 1)
    owner = jnp.where(j < 128, lev, 1 - lev)
    down[...] = fill(i % LEV, owner * LEVD + j % LEVD, i // LEV == (j // LEVD) % 2)


def make_spread(pair_s, me, spread):
    for k in range(ROUNDS):
        a, b = WINDOWS[k]
        low, high, split, _ = round_scalars(pair_s, me, k)
        rows = a + iota((1, b - a), 1)
        degree = jnp.where(rows < split, rows + (low - PIECES[k][0]), rows + (high - split)).astype(F32)
        value = degree * (degree + 1.0) / float(M * M)
        if k > 0:
            width = 128
            first = jnp.where(rows[:, :width] < PIECES[k][0], spread[0:1, a : a + width], value[:, :width])
            spread[0:1, a : a + width] = first
            if b - a > width:
                spread[0:1, a + width : b] = value[:, width:]
        else:
            spread[0:1, a:b] = value


def make_table(pair_v, table):
    lane = iota((128, 128), 1).astype(F32)
    for ch in range(CHUNKS):
        pairs = [jnp.broadcast_to(pair_v[:, 2 * ch + kk : 2 * ch + kk + 1], (NW, 128)) for kk in range(2)]
        pair = jnp.concatenate(pairs, axis=0)
        base = 2 * NW * (2 * ch + iota((128, 128), 0) // NW)
        low, high = base + pair, base + 2 * NW - 1 - pair
        even = pair % 2 == 0
        for par in range(2):
            wave = (jnp.where(even, low, high) if par == 0 else jnp.where(even, high, low)).astype(F32)
            c, s = cos_sin(wave * lane, NLON)
            c, s = c * NLON ** -0.5, s * NLON ** -0.5
            rc, rs = cos_sin(wave * 128.0, NLON)
            for b in range(TILES):
                lanes = slice(b * 128, (b + 1) * 128)
                if b == TILES - 1:
                    c, s = jnp.where(lane < HALF - 128.0 * b, c, 0.0), jnp.where(lane < HALF - 128.0 * b, s, 0.0)
                table[par, ch, 0:128, lanes] = c.astype(BF)
                table[par, ch, 128:256, lanes] = (-s).astype(BF)
                if b < TILES - 1:
                    c, s = c * rc - s * rs, s * rc + c * rs


def gather_spectra(sx, par):
    return jnp.concatenate(
        [
            jnp.concatenate(
                [
                    sx[pl.ds(kk * 8 + r * 4 + slot * 2 + par, NW, stride=16), :]
                    for r in range(2)
                    for kk in range(2)
                ],
                axis=0,
            )
            for slot in range(2)
        ],
        axis=1,
    ).astype(BF)


def synthesize(x, table, sx, acc, ch):
    sx[...] = x.astype(F32).reshape(NW * 16, 128)
    for par in range(2):
        part = mm(gather_spectra(sx, par), table[par, ch], TN)
        if ch == 0:
            acc[par] = part
        else:
            acc[par] = acc[par] + part


def slot_terms(acc, slot):
    base = slot * 128
    eu, ev = acc[0, base : base + 64, :], acc[0, base + 64 : base + 128, :]
    ou, ov = acc[1, base : base + 64, :], acc[1, base + 64 : base + 128, :]
    out = []
    for u, v in ((eu + ou, ev + ov), (eu - ou, ev - ov)):
        out.append(((-4.0 * u * v).astype(BF), (2.0 * (u * u - v * v)).astype(BF)))
    return out


def store_band(band, slot, f, first, second, keep):
    p = jnp.where(keep, first.astype(F32), 0.0)
    q = jnp.where(keep, second.astype(F32), 0.0)
    rolled = pltpu.roll(q, 64, axis=1)
    band[slot, f, :, 0:1280] = p[:, 0:1280].astype(BF)
    band[slot, f, :, 1280:1408] = (p[:, 1280:1408] + rolled[:, 0:128]).astype(BF)
    band[slot, f, :, 1408:2688] = rolled[:, 128:1408].astype(BF)


def body(
    pair_s, rows_s, pair_v, rows_v, weights_v, rates_v, state, basis,
    new, band,
    other, table, st_a, st_b, st_c, rv_a, rv_b, rv_c, rv_p, sx, sy, acc, tp, pick, up, down, spread,
    send_sem, ra_sem, rb_sem, rc_sem, rp_sem, state_sem, own_sem,
):
    me = lax.axis_index("wave")
    lev = lax.axis_index("lev")
    z, y, x = me // 16, (me // 4) % 4, me % 4
    across = 1 - lev

    def each_peer(action):
        for dx in range(1, 4):
            action(z * 16 + y * 4 + (x + dx) % 4)

        def step(i, carry):
            at = (z + i // 4) % 4 * 16 + (y + i % 4) % 4 * 4
            for dx in range(4):
                action(at + (x + dx) % 4)
            return carry

        lax.fori_loop(1, 16, step, 0)

    barrier = pltpu.get_barrier_semaphore()
    each_peer(lambda p: pl.semaphore_signal(barrier, inc=1, device_id={"wave": p}, device_id_type=MESH))
    pl.semaphore_signal(barrier, inc=1, device_id={"lev": across}, device_id_type=MESH)

    make_picks(rows_v, pick)
    make_modes(lev, up, down)
    make_spread(pair_s, me, spread)

    pl.semaphore_wait(barrier, NW)
    swap = pltpu.make_async_remote_copy(
        src_ref=state, dst_ref=other, send_sem=state_sem.at[0], recv_sem=state_sem.at[1],
        device_id={"lev": across}, device_id_type=MESH,
    )
    swap.start()

    def send(stage, land, sems, which, ch):
        pltpu.make_async_copy(stage.at[ch, me], land.at[ch, me], own_sem.at[which, ch]).start()

        def one(p):
            pltpu.make_async_remote_copy(
                src_ref=stage.at[ch, p], dst_ref=land.at[ch, me], send_sem=send_sem.at[which, ch],
                recv_sem=sems.at[ch], device_id={"wave": p}, device_id_type=MESH,
            ).start()

        each_peer(one)

    def many(stage, land, sems, which, ch):
        return pltpu.make_async_remote_copy(
            src_ref=stage.at[ch, pl.ds(0, NW - 1)], dst_ref=land.at[ch, pl.ds(0, NW - 1)],
            send_sem=send_sem.at[which, ch], recv_sem=sems.at[ch], device_id={"wave": me}, device_id_type=MESH,
        )

    def arrive(stage, land, sems, which, ch):
        pltpu.make_async_copy(stage.at[ch, me], land.at[ch, me], own_sem.at[which, ch]).wait()
        many(stage, land, sems, which, ch).wait_recv()

    for ch in range(CHUNKS):
        for kk in range(2):
            k = 2 * ch + kk
            a, b = WINDOWS[k]
            low, _, _, ranges = round_scalars(pair_s, me, k)
            both = masked_basis(basis, ranges, k)
            rows = jnp.concatenate([state[c, :, a:b] for c in (0, 2, 1, 3)], axis=0)
            product = mm(rows, both, NN)
            for par in range(2):
                part = product[:, par * LAT : (par + 1) * LAT]
                if k == 0 and par == 0:
                    part = part * jnp.where(low == 0, 0.5, 1.0)
                picked = mm(pick[...], part.astype(BF), NT)
                for r in range(2):
                    lanes = slice(r * 128, (r + 1) * 128)
                    for slot in range(2):
                        at = kk * 8 + r * 4 + slot * 2 + par
                        sx[pl.ds(at, NW, stride=16), :] = picked[slot * NW : (slot + 1) * NW, lanes]
                        sy[pl.ds(at, NW, stride=16), :] = picked[(2 + slot) * NW : (3 + slot) * NW, lanes]
        st_a[ch] = sx[...].reshape(NW, 16, 128).astype(BF)
        st_b[ch] = sy[...].reshape(NW, 16, 128).astype(BF)
        send(st_a, rv_a, ra_sem, 0, ch)

    for ch in range(CHUNKS):
        send(st_b, rv_b, rb_sem, 1, ch)

    make_table(pair_v, table)

    for ch in range(CHUNKS):
        arrive(st_a, rv_a, ra_sem, 0, ch)
        synthesize(rv_a[ch], table, sx, acc, ch)

    rows_mine = rows_s[me]
    for slot in range(2):
        first, second = slot_terms(acc, slot)
        for f in range(2):
            at = slot * 128 + f * 64
            p, q = first[f].astype(F32), second[f].astype(F32)
            tp[0, at : at + 64, :] = (p + q).astype(BF)
            tp[1, at : at + 64, :] = (p - q).astype(BF)
            store_band(band, slot, f, first[f], second[f], rows_mine > slot)

    slot_row = iota((2 * NW, LAT), 0)
    weight = [
        jnp.sum(
            jnp.where(slot_row == slot * NW + me, pick[0 : 2 * NW, :].astype(F32) * weights_v[...], 0.0),
            axis=(0, 1), keepdims=True,
        )
        for slot in range(2)
    ]
    for ch in range(CHUNKS):
        for par in range(2):
            coeff = mm(table[par, ch], tp[par], NT).astype(BF).astype(F32)
            for slot in range(2):
                part = coeff[:, slot * 128 : (slot + 1) * 128] * weight[slot]
                for r in range(2):
                    for kk in range(2):
                        at = r * 128 + kk * NW
                        sx[pl.ds(kk * 8 + r * 4 + slot * 2 + par, NW, stride=16), :] = part[at : at + NW]
        st_c[ch] = sx[...].reshape(NW, 16, 128).astype(BF)
        send(st_c, rv_c, rc_sem, 2, ch)

    swap.wait_recv()
    tile = HPAD
    for a in range(0, NR, tile):
        b = min(a + tile, NR)
        factor = 1.0 / (1.0 + rates_v[...] * spread[0:1, a:b])
        factor = jnp.concatenate([factor, factor], axis=0)
        for r in range(2):
            levels = jnp.concatenate(
                [state[r, :, a:b], state[2 + r, :, a:b], other[r, :, a:b], other[2 + r, :, a:b]], axis=0
            )
            modes = (mm(down[...], levels, NN) * factor).astype(BF)
            result = mm(up[...], modes, NN).astype(BF)
            new[r, :, a:b] = result[0:64]
            new[2 + r, :, a:b] = result[64:128]

    for ch in range(CHUNKS):
        arrive(st_b, rv_b, rb_sem, 1, ch)
        synthesize(rv_b[ch], table, sx, acc, ch)
    for slot in range(2):
        first, second = slot_terms(acc, slot)
        for f in range(2):
            store_band(band, 2 + slot, f, first[f], second[f], rows_mine > 2 + slot)

    def forward(ch):
        return pltpu.make_async_remote_copy(
            src_ref=rv_c.at[ch], dst_ref=rv_p.at[ch], send_sem=send_sem.at[3, ch], recv_sem=rp_sem.at[ch],
            device_id={"lev": across}, device_id_type=MESH,
        )

    for ch in range(CHUNKS):
        arrive(st_c, rv_c, rc_sem, 2, ch)
        forward(ch).start()
    for ch in range(CHUNKS):
        forward(ch).wait_recv()
        sx[...] = rv_c[ch].astype(F32).reshape(NW * 16, 128)
        sy[...] = rv_p[ch].astype(F32).reshape(NW * 16, 128)
        for kk in range(2):
            k = 2 * ch + kk
            a, b = WINDOWS[k]
            _, _, _, ranges = round_scalars(pair_s, me, k)
            both = masked_basis(basis, ranges, k)
            factor = STEP_WEIGHT / (1.0 + rates_v[...] * spread[0:1, a:b])
            factor = jnp.concatenate([factor, factor], axis=0)
            for r in range(2):
                weighted = []
                for par in range(2):
                    at = [kk * 8 + r * 4 + slot * 2 + par for slot in range(2)]
                    gathered = jnp.concatenate(
                        [jnp.concatenate([s[pl.ds(i, NW, stride=16), :] for i in at], axis=0) for s in (sx, sy)],
                        axis=1,
                    ).astype(BF)
                    by_lat = mm(pick[0 : 2 * NW, :], gathered, TN).astype(BF)
                    weighted.append(mm(by_lat, down[...], NT).astype(BF))
                pair = jnp.concatenate(weighted, axis=0)
                modes = (mm(pair, both, TT) * factor).astype(BF)
                change = mm(up[...], modes, NN)
                for f in range(2):
                    c = 2 * f + r
                    new[c, :, a:b] = (new[c, :, a:b].astype(F32) + change[f * 64 : (f + 1) * 64]).astype(BF)

    swap.wait_send()
    for which, (stage, land, sems) in enumerate(((st_a, rv_a, ra_sem), (st_b, rv_b, rb_sem), (st_c, rv_c, rc_sem))):
        for ch in range(CHUNKS):
            many(stage, land, sems, which, ch).wait_send()
    for ch in range(CHUNKS):
        forward(ch).wait_send()


def local(spectral_state, legendre_basis, pairing, band_rows, weights, mode_rates):
    vmem = pl.BlockSpec(memory_space=pltpu.VMEM)
    smem = pl.BlockSpec(memory_space=pltpu.SMEM)
    stage = pltpu.VMEM((CHUNKS, NW, 16, 128), BF)
    work = pltpu.VMEM((NW * 16, 128), F32)
    sems = pltpu.SemaphoreType.DMA((CHUNKS,))
    return pl.pallas_call(
        body,
        out_shape=(
            jax.ShapeDtypeStruct((4, LEVD, NR), BF),
            jax.ShapeDtypeStruct((4, 2, LEVD, NLON), BF),
        ),
        in_specs=[smem] * 2 + [vmem] * 6,
        out_specs=(vmem, vmem),
        scratch_shapes=[
            pltpu.VMEM((4, LEVD, NR), BF),
            pltpu.VMEM((2, CHUNKS, 256, HPAD), BF),
            stage, stage, stage, stage, stage, stage, stage,
            work, work,
            pltpu.VMEM((2, 256, HPAD), F32),
            pltpu.VMEM((2, 256, HPAD), BF),
            pltpu.VMEM((256, 128), BF),
            pltpu.VMEM((128, 256), BF),
            pltpu.VMEM((256, 256), BF),
            pltpu.VMEM((8, NR), F32),
            pltpu.SemaphoreType.DMA((4, CHUNKS)),
            sems, sems, sems, sems,
            pltpu.SemaphoreType.DMA((2,)),
            pltpu.SemaphoreType.DMA((3, CHUNKS)),
        ],
        compiler_params=pltpu.CompilerParams(
            collective_id=0, has_side_effects=True, vmem_limit_bytes=VMEM_LIMIT
        ),
    )(
        pairing, band_rows, pairing, band_rows[None, :], weights[None, :], mode_rates[:, None],
        spectral_state, legendre_basis,
    )


def solution(mesh):
    in_specs = (P(None, "lev", "wave"), P("wave", None), P(), P(), P(), P())
    out_specs = (P(None, "lev", "wave"), P("wave", None, "lev", None))
    return jax.shard_map(local, mesh=mesh, in_specs=in_specs, out_specs=out_specs, check_vma=False)
```

```python
import math

import jax
import jax.numpy as jnp
from jax import lax
from jax.experimental import pallas as pl
from jax.experimental.pallas import tpu as pltpu
from jax.sharding import PartitionSpec as P

M = 1280
NLON = 2688
HALF = NLON // 2
TILES = 11
HPAD = 128 * TILES
LAT = 128
NW = 64
NR = 12810
LEV = 128
LEVD = 64
ROUNDS = M // (2 * NW)
CHUNKS = ROUNDS // 2
PIECES = []
_offset = 0
for _k in range(ROUNDS):
    _length = 2 * M - 4 * _k * NW - 2 * NW + 1
    PIECES.append((_offset, _length))
    _offset += _length
GROUPS = ((0, 1), (1, 2), (3, 2))
EXTRA = ((0, CHUNKS),)
WINDOWS = [(o // 128 * 128, min(-(-(o + n) // 128) * 128, NR)) for o, n in PIECES]
STEP_WEIGHT = 0.5
VMEM_LIMIT = 61 * 1024 * 1024
BF = jnp.bfloat16
F32 = jnp.float32
I32 = jnp.int32
MESH = pl.DeviceIdType.MESH
NN = (((1,), (0,)), ((), ()))
NT = (((1,), (1,)), ((), ()))
TN = (((0,), (0,)), ((), ()))


def mm(a, b, dims):
    return lax.dot_general(a, b, dims, preferred_element_type=F32)


def iota(shape, dim):
    return lax.broadcasted_iota(I32, shape, dim)


def cos_sin(turns, period):
    rest = turns - jnp.floor(turns * (1.0 / period) + 0.5) * float(period)
    y = rest * (math.pi / period)
    z = y * y
    s = -1.0 / 39916800.0
    for term in (1.0 / 362880.0, -1.0 / 5040.0, 1.0 / 120.0, -1.0 / 6.0, 1.0):
        s = s * z + term
    s = s * y
    c = 1.0 / 479001600.0
    for term in (-1.0 / 3628800.0, 1.0 / 40320.0, -1.0 / 720.0, 1.0 / 24.0, -0.5, 1.0):
        c = c * z + term
    return 1.0 - 2.0 * s * s, 2.0 * s * c


def round_scalars(pair_mine, k):
    pair = pair_mine[:, k : k + 1]
    begin, length = PIECES[k]
    low = 2 * NW * k + pair
    high = 2 * NW * k + 2 * NW - 1 - pair
    split = begin + M - low
    even = pair % 2 == 0
    end = begin + length
    ranges = (
        jnp.where(even, begin, split),
        jnp.where(even, split, end),
        jnp.where(even, split, begin),
        jnp.where(even, end, split),
    )
    return low, high, split, ranges


def masked_basis(basis, ranges, k):
    a, b = WINDOWS[k]
    rows = a + iota((b - a, 1), 0)
    block = basis[a:b, :].astype(F32)
    even = (rows >= ranges[0]) & (rows < ranges[1])
    odd = (rows >= ranges[2]) & (rows < ranges[3])
    return jnp.concatenate(
        [jnp.where(even, block, 0.0).astype(BF), jnp.where(odd, block, 0.0).astype(BF)], axis=1
    )


def masked_across(flipped, ranges, k):
    a, b = WINDOWS[k]
    rows = a + iota((1, b - a), 1)
    block = flipped[:, a:b].astype(F32)
    even = (rows >= ranges[0]) & (rows < ranges[1])
    odd = (rows >= ranges[2]) & (rows < ranges[3])
    return jnp.concatenate(
        [jnp.where(even, block, 0.0).astype(BF), jnp.where(odd, block, 0.0).astype(BF)], axis=0
    )


def make_picks(rows_v, pick):
    d = iota((NW, NW), 0)
    e = iota((NW, NW), 1)
    count_row = rows_v[...]
    before = e < d
    count = jnp.sum(jnp.where(e == d, count_row, 0).astype(F32), axis=1, keepdims=True)
    starts = jnp.sum(jnp.where(before, count_row, 0).astype(F32), axis=1, keepdims=True)
    single_rank = jnp.sum(jnp.where(before & (count_row == 1), 1.0, 0.0), axis=1, keepdims=True)
    lat = iota((NW, LAT), 1).astype(F32)
    hit = (starts <= lat) & (lat < starts + count)
    slot = jnp.sum(jnp.where(hit, lat - starts, 0.0), axis=0, keepdims=True)
    extra = jnp.where(slot >= 1.5, 1.0, 0.0)
    ahead = jnp.where(iota((LAT, LAT), 0) < iota((LAT, LAT), 1), 1.0, 0.0).astype(BF)
    extra8 = jnp.broadcast_to(extra, (16, LAT)).astype(BF)
    rank = mm(extra8, ahead, NN)[0:1, :]
    adopted = (extra > 0.5) & (rank == single_rank)
    second = jnp.where(count < 1.5, jnp.where(adopted, 1.0, 0.0), jnp.where(lat == starts + 1.0, 1.0, 0.0))
    pick[0:NW, :] = jnp.where(lat == starts, 1.0, 0.0).astype(BF)
    pick[NW : 2 * NW, :] = second.astype(BF)
    pick[2 * NW : 3 * NW, :] = jnp.where(lat == starts + 2.0, 1.0, 0.0).astype(BF)
    pick[3 * NW : 4 * NW, :] = jnp.where(lat == starts + 3.0, 1.0, 0.0).astype(BF)


def make_modes(lev, up, down):
    def fill(mode_index, level_index, same):
        phase = ((2 * level_index + 1) * mode_index).astype(F32)
        cosine, _ = cos_sin(phase, 4 * LEV)
        scale = jnp.where(mode_index == 0, math.sqrt(1.0 / LEV), math.sqrt(2.0 / LEV))
        return jnp.where(same, cosine * scale, 0.0).astype(BF)

    i, j = iota((128, 256), 0), iota((128, 256), 1)
    up[...] = fill(j % LEV, lev * LEVD + i % LEVD, i // LEVD == j // LEV)
    i, j = iota((256, 256), 0), iota((256, 256), 1)
    owner = jnp.where(j < 128, lev, 1 - lev)
    down[...] = fill(i % LEV, owner * LEVD + j % LEVD, i // LEV == (j // LEVD) % 2)


def make_spread(pair_mine, spread):
    for k in range(ROUNDS):
        a, b = WINDOWS[k]
        low, high, split, _ = round_scalars(pair_mine, k)
        rows = a + iota((1, b - a), 1)
        degree = jnp.where(rows < split, rows + (low - PIECES[k][0]), rows + (high - split)).astype(F32)
        value = degree * (degree + 1.0) / float(M * M)
        if k > 0:
            width = 128
            first = jnp.where(rows[:, :width] < PIECES[k][0], spread[0:1, a : a + width], value[:, :width])
            spread[0:1, a : a + width] = first
            if b - a > width:
                spread[0:1, a + width : b] = value[:, width:]
        else:
            spread[0:1, a:b] = value


def make_table(pair_v, table):
    lane = iota((128, 128), 1).astype(F32)
    for ch in range(CHUNKS):
        pairs = [jnp.broadcast_to(pair_v[:, 2 * ch + kk : 2 * ch + kk + 1], (NW, 128)) for kk in range(2)]
        pair = jnp.concatenate(pairs, axis=0)
        base = 2 * NW * (2 * ch + iota((128, 128), 0) // NW)
        low, high = base + pair, base + 2 * NW - 1 - pair
        even = pair % 2 == 0
        for par in range(2):
            wave = (jnp.where(even, low, high) if par == 0 else jnp.where(even, high, low)).astype(F32)
            c, s = cos_sin(wave * lane, NLON)
            c, s = c * NLON ** -0.5, s * NLON ** -0.5
            rc, rs = cos_sin(wave * 128.0, NLON)
            for b in range(TILES):
                lanes = slice(b * 128, (b + 1) * 128)
                if b == TILES - 1:
                    c, s = jnp.where(lane < HALF - 128.0 * b, c, 0.0), jnp.where(lane < HALF - 128.0 * b, s, 0.0)
                table[par, ch, 0:128, lanes] = c.astype(BF)
                table[par, ch, 128:256, lanes] = (-s).astype(BF)
                if b < TILES - 1:
                    c, s = c * rc - s * rs, s * rc + c * rs


def gather_spectra(sx, par):
    return jnp.concatenate(
        [
            jnp.concatenate(
                [
                    sx[pl.ds(kk * 8 + r * 4 + slot * 2 + par, NW, stride=16), :]
                    for r in range(2)
                    for kk in range(2)
                ],
                axis=0,
            )
            for slot in range(2)
        ],
        axis=1,
    ).astype(BF)


def synthesize(x, table, sx, acc, ch):
    sx[...] = x.astype(F32).reshape(NW * 16, 128)
    for par in range(2):
        part = mm(gather_spectra(sx, par), table[par, ch], TN)
        if ch == 0:
            acc[par] = part
        else:
            acc[par] = acc[par] + part


def slot_terms(acc, slot):
    base = slot * 128
    eu, ev = acc[0, base : base + 64, :], acc[0, base + 64 : base + 128, :]
    ou, ov = acc[1, base : base + 64, :], acc[1, base + 64 : base + 128, :]
    out = []
    for u, v in ((eu + ou, ev + ov), (eu - ou, ev - ov)):
        out.append(((-4.0 * u * v).astype(BF), (2.0 * (u * u - v * v)).astype(BF)))
    return out


def store_band(band, slot, f, first, second, keep):
    p = jnp.where(keep, first.astype(F32), 0.0)
    q = jnp.where(keep, second.astype(F32), 0.0)
    rolled = pltpu.roll(q, 64, axis=1)
    band[slot, f, :, 0:1280] = p[:, 0:1280].astype(BF)
    band[slot, f, :, 1280:1408] = (p[:, 1280:1408] + rolled[:, 0:128]).astype(BF)
    band[slot, f, :, 1408:2688] = rolled[:, 128:1408].astype(BF)


def body(
    pair_v, rows_v, weights_v, rates_v, state_in, basis_in,
    new_out, band_out,
    state, basis, flipped, band, other, table, st_a, st_b, st_c, rv_a, rv_b, rv_c, rv_p, sx, sy, acc, tp,
    pick, up, down, spread, rates,
    send_sem, ra_sem, rb_sem, rc_sem, rp_sem, state_sem, own_sem, io_sem,
):
    me = lax.axis_index("wave")
    lev = lax.axis_index("lev")
    z, y, x = me // 16, (me // 4) % 4, me % 4
    across = 1 - lev

    load_state = pltpu.make_async_copy(state_in, state, io_sem.at[0])
    load_basis = pltpu.make_async_copy(basis_in, basis, io_sem.at[1])
    load_state.start()
    load_basis.start()

    def each_peer(action):
        for dx in range(1, 4):
            action(z * 16 + y * 4 + (x + dx) % 4)

        def step(i, carry):
            at = (z + i // 4) % 4 * 16 + (y + i % 4) % 4 * 4
            for dx in range(4):
                action(at + (x + dx) % 4)
            return carry

        lax.fori_loop(1, 16, step, 0)

    barrier = pltpu.get_barrier_semaphore()
    each_peer(lambda p: pl.semaphore_signal(barrier, inc=1, device_id={"wave": p}, device_id_type=MESH))
    pl.semaphore_signal(barrier, inc=1, device_id={"lev": across}, device_id_type=MESH)

    mine = iota((NW, ROUNDS), 0) == me
    pair_mine = jnp.sum(jnp.where(mine, pair_v[...], 0).astype(F32), axis=0, keepdims=True).astype(I32)
    make_picks(rows_v, pick)
    make_modes(lev, up, down)
    make_spread(pair_mine, spread)
    diagonal = iota((LEV, LEV), 0) == iota((LEV, LEV), 1)
    rates[...] = jnp.sum(jnp.where(diagonal, rates_v[...], 0.0), axis=1, keepdims=True)
    rows_mine = jnp.sum(
        jnp.where(iota((1, NW), 1) == me, rows_v[...], 0).astype(F32), axis=1, keepdims=True
    )

    pl.semaphore_wait(barrier, NW)
    swap = pltpu.make_async_remote_copy(
        src_ref=state_in, dst_ref=other, send_sem=state_sem.at[0], recv_sem=state_sem.at[1],
        device_id={"lev": across}, device_id_type=MESH,
    )

    def own(stage, land, which, g, group):
        at = pl.ds(group[0], group[1])
        return pltpu.make_async_copy(stage.at[at, me], land.at[at, me], own_sem.at[which, g])

    def send(stage, land, sems, which, g, group):
        at = pl.ds(group[0], group[1])
        own(stage, land, which, g, group).start()

        def one(p):
            pltpu.make_async_remote_copy(
                src_ref=stage.at[at, p], dst_ref=land.at[at, me], send_sem=send_sem.at[which, g],
                recv_sem=sems.at[g], device_id={"wave": p}, device_id_type=MESH,
            ).start()

        each_peer(one)

    def many(stage, land, sems, which, g, group):
        at = (pl.ds(group[0], group[1]), pl.ds(0, NW - 1))
        return pltpu.make_async_remote_copy(
            src_ref=stage.at[at], dst_ref=land.at[at],
            send_sem=send_sem.at[which, g], recv_sem=sems.at[g], device_id={"wave": me}, device_id_type=MESH,
        )

    def arrive(stage, land, sems, which, g, group):
        own(stage, land, which, g, group).wait()
        many(stage, land, sems, which, g, group).wait_recv()

    load_basis.wait()
    load_state.wait()
    for g, group in enumerate(GROUPS):
        for ch in range(group[0], sum(group)):
            for kk in range(2):
                k = 2 * ch + kk
                a, b = WINDOWS[k]
                low, _, _, ranges = round_scalars(pair_mine, k)
                both = masked_basis(basis, ranges, k)
                rows = jnp.concatenate([state[c, :, a:b] for c in (0, 2, 1, 3)], axis=0)
                product = mm(rows, both, NN)
                for par in range(2):
                    part = product[:, par * LAT : (par + 1) * LAT]
                    if k == 0 and par == 0:
                        part = part * jnp.where(low == 0, 0.5, 1.0)
                    picked = mm(pick[...], part.astype(BF), NT)
                    for r in range(2):
                        lanes = slice(r * 128, (r + 1) * 128)
                        for slot in range(2):
                            at = kk * 8 + r * 4 + slot * 2 + par
                            sx[pl.ds(at, NW, stride=16), :] = picked[slot * NW : (slot + 1) * NW, lanes]
                            sy[pl.ds(at, NW, stride=16), :] = picked[(2 + slot) * NW : (3 + slot) * NW, lanes]
            st_a[ch] = sx[...].reshape(NW, 16, 128).astype(BF)
            st_b[ch] = sy[...].reshape(NW, 16, 128).astype(BF)
        send(st_a, rv_a, ra_sem, 0, g, group)
        if g == 0:
            swap.start()

    send(st_b, rv_b, rb_sem, 1, 0, EXTRA[0])

    make_table(pair_v, table)
    tile = HPAD
    unit = jnp.where(diagonal, 1.0, 0.0).astype(BF)
    for a in range(0, NR, tile):
        b = min(a + tile, NR)
        flipped[:, a:b] = mm(unit, basis[a:b, :], NT).astype(BF)

    def couple(first, last):
        for a in range(first * tile, min(last * tile, NR), tile):
            b = min(a + tile, NR)
            factor = 1.0 / (1.0 + rates[...] * spread[0:1, a:b])
            factor = jnp.concatenate([factor, factor], axis=0)
            for r in range(2):
                levels = jnp.concatenate(
                    [state[r, :, a:b], state[2 + r, :, a:b], other[r, :, a:b], other[2 + r, :, a:b]], axis=0
                )
                modes = (mm(down[...], levels, NN) * factor).astype(BF)
                result = mm(up[...], modes, NN).astype(BF)
                state[r, :, a:b] = result[0:64]
                state[2 + r, :, a:b] = result[64:128]

    swap.wait_recv()
    couple(0, 5)

    for g, group in enumerate(GROUPS):
        arrive(st_a, rv_a, ra_sem, 0, g, group)
        for ch in range(group[0], sum(group)):
            synthesize(rv_a[ch], table, sx, acc, ch)

    for slot in range(2):
        first, second = slot_terms(acc, slot)
        for f in range(2):
            at = slot * 128 + f * 64
            p, q = first[f].astype(F32), second[f].astype(F32)
            tp[0, at : at + 64, :] = (p + q).astype(BF)
            tp[1, at : at + 64, :] = (p - q).astype(BF)
            store_band(band, slot, f, first[f], second[f], rows_mine > slot + 0.5)
    save_home = pltpu.make_async_copy(band.at[pl.ds(0, 2)], band_out.at[pl.ds(0, 2)], io_sem.at[2])
    save_extra = pltpu.make_async_copy(band.at[pl.ds(2, 2)], band_out.at[pl.ds(2, 2)], io_sem.at[3])
    save_home.start()

    slot_row = iota((2 * NW, LAT), 0)
    weight = [
        jnp.sum(
            jnp.where(slot_row == slot * NW + me, pick[0 : 2 * NW, :].astype(F32) * weights_v[...], 0.0),
            axis=(0, 1), keepdims=True,
        )
        for slot in range(2)
    ]
    for g, group in enumerate(GROUPS):
        for ch in range(group[0], sum(group)):
            for par in range(2):
                coeff = mm(table[par, ch], tp[par], NT).astype(BF).astype(F32)
                for slot in range(2):
                    part = coeff[:, slot * 128 : (slot + 1) * 128] * weight[slot]
                    for r in range(2):
                        for kk in range(2):
                            at = r * 128 + kk * NW
                            sx[pl.ds(kk * 8 + r * 4 + slot * 2 + par, NW, stride=16), :] = part[at : at + NW]
            st_c[ch] = sx[...].reshape(NW, 16, 128).astype(BF)
        send(st_c, rv_c, rc_sem, 2, g, group)

    couple(5, 10)

    arrive(st_b, rv_b, rb_sem, 1, 0, EXTRA[0])
    for ch in range(CHUNKS):
        synthesize(rv_b[ch], table, sx, acc, ch)
    for slot in range(2):
        first, second = slot_terms(acc, slot)
        for f in range(2):
            store_band(band, 2 + slot, f, first[f], second[f], rows_mine > slot + 2.5)
    save_extra.start()

    def forward(g, group):
        at = pl.ds(group[0], group[1])
        return pltpu.make_async_remote_copy(
            src_ref=rv_c.at[at], dst_ref=rv_p.at[at], send_sem=send_sem.at[3, g], recv_sem=rp_sem.at[g],
            device_id={"lev": across}, device_id_type=MESH,
        )

    saves = []

    def direct(g, group):
        forward(g, group).wait_recv()
        for ch in range(group[0], sum(group)):
            sx[...] = rv_c[ch].astype(F32).reshape(NW * 16, 128)
            sy[...] = rv_p[ch].astype(F32).reshape(NW * 16, 128)
            for kk in range(2):
                k = 2 * ch + kk
                a, b = WINDOWS[k]
                _, _, _, ranges = round_scalars(pair_mine, k)
                both = masked_across(flipped, ranges, k)
                factor = STEP_WEIGHT / (1.0 + rates[...] * spread[0:1, a:b])
                factor = jnp.concatenate([factor, factor], axis=0)
                for r in range(2):
                    weighted = []
                    for par in range(2):
                        at = [kk * 8 + r * 4 + slot * 2 + par for slot in range(2)]
                        gathered = jnp.concatenate(
                            [
                                jnp.concatenate([s[pl.ds(i, NW, stride=16), :] for i in at], axis=0)
                                for s in (sx, sy)
                            ],
                            axis=1,
                        ).astype(BF)
                        by_lat = mm(pick[0 : 2 * NW, :], gathered, TN).astype(BF)
                        weighted.append(mm(by_lat, down[...], NT).astype(BF))
                    pair = jnp.concatenate(weighted, axis=0)
                    modes = (mm(pair, both, TN) * factor).astype(BF)
                    change = mm(up[...], modes, NN)
                    for f in range(2):
                        c = 2 * f + r
                        state[c, :, a:b] = (
                            state[c, :, a:b].astype(F32) + change[f * 64 : (f + 1) * 64]
                        ).astype(BF)
        a = WINDOWS[2 * group[0]][0]
        if g < len(GROUPS) - 1:
            b = WINDOWS[2 * sum(group)][0]
            at = (pl.ds(0, 4), pl.ds(0, LEVD), pl.ds(a, b - a))
        else:
            at = (pl.ds(0, 4), pl.ds(0, LEVD), pl.ds(a, NR - a))
        save = pltpu.make_async_copy(state.at[at], new_out.at[at], io_sem.at[4 + g])
        save.start()
        saves.append(save)

    for g, group in enumerate(GROUPS):
        arrive(st_c, rv_c, rc_sem, 2, g, group)
        forward(g, group).start()
        if g > 0:
            direct(g - 1, GROUPS[g - 1])
    direct(len(GROUPS) - 1, GROUPS[-1])

    swap.wait_send()
    for g, group in enumerate(GROUPS):
        many(st_a, rv_a, ra_sem, 0, g, group).wait_send()
        many(st_c, rv_c, rc_sem, 2, g, group).wait_send()
        forward(g, group).wait_send()
    many(st_b, rv_b, rb_sem, 1, 0, EXTRA[0]).wait_send()
    save_home.wait()
    save_extra.wait()
    for save in saves:
        save.wait()


def local(spectral_state, legendre_basis, pairing, band_rows, weights, mode_rates):
    vmem = pl.BlockSpec(memory_space=pltpu.VMEM)
    anywhere = pl.BlockSpec(memory_space=pl.ANY)
    stage = pltpu.VMEM((CHUNKS, NW, 16, 128), BF)
    work = pltpu.VMEM((NW * 16, 128), F32)
    sems = pltpu.SemaphoreType.DMA((len(GROUPS),))
    return pl.pallas_call(
        body,
        out_shape=(
            jax.ShapeDtypeStruct((4, LEVD, NR), BF),
            jax.ShapeDtypeStruct((4, 2, LEVD, NLON), BF),
        ),
        in_specs=[vmem] * 4 + [anywhere] * 2,
        out_specs=(anywhere, anywhere),
        scratch_shapes=[
            pltpu.VMEM((4, LEVD, NR), BF),
            pltpu.VMEM((NR, LAT), BF),
            pltpu.VMEM((LAT, NR), BF),
            pltpu.VMEM((4, 2, LEVD, NLON), BF),
            pltpu.VMEM((4, LEVD, NR), BF),
            pltpu.VMEM((2, CHUNKS, 256, HPAD), BF),
            stage, stage, stage, stage, stage, stage, stage,
            work, work,
            pltpu.VMEM((2, 256, HPAD), F32),
            pltpu.VMEM((2, 256, HPAD), BF),
            pltpu.VMEM((256, 128), BF),
            pltpu.VMEM((128, 256), BF),
            pltpu.VMEM((256, 256), BF),
            pltpu.VMEM((8, NR), F32),
            pltpu.VMEM((LEV, 1), F32),
            pltpu.SemaphoreType.DMA((4, len(GROUPS))),
            sems, sems, sems, sems,
            pltpu.SemaphoreType.DMA((2,)),
            pltpu.SemaphoreType.DMA((3, len(GROUPS))),
            pltpu.SemaphoreType.DMA((4 + len(GROUPS),)),
        ],
        compiler_params=pltpu.CompilerParams(
            collective_id=0, has_side_effects=True, vmem_limit_bytes=VMEM_LIMIT
        ),
    )(
        pairing, band_rows[None, :], weights[None, :], mode_rates[None, :], spectral_state, legendre_basis,
    )


def solution(mesh):
    in_specs = (P(None, "lev", "wave"), P("wave", None), P(), P(), P(), P())
    out_specs = (P(None, "lev", "wave"), P("wave", None, "lev", None))
    return jax.shard_map(local, mesh=mesh, in_specs=in_specs, out_specs=out_specs, check_vma=False)
```

```python
import math

import jax
import jax.numpy as jnp
from jax import lax
from jax.experimental import pallas as pl
from jax.experimental.pallas import tpu as pltpu
from jax.sharding import PartitionSpec as P

M = 1280
NLON = 2688
HALF = NLON // 2
TILES = 11
HPAD = 128 * TILES
LAT = 128
NW = 64
NR = 12810
LEV = 128
LEVD = 64
ROUNDS = M // (2 * NW)
CHUNKS = ROUNDS // 2
PIECES = []
_offset = 0
for _k in range(ROUNDS):
    _length = 2 * M - 4 * _k * NW - 2 * NW + 1
    PIECES.append((_offset, _length))
    _offset += _length
GROUPS = ((0, 1), (1, 2), (3, 2))
EXTRA = ((0, CHUNKS),)
LAST = GROUPS[-1][0]
WINDOWS = [(o // 128 * 128, min(-(-(o + n) // 128) * 128, NR)) for o, n in PIECES]
TAIL = WINDOWS[2 * LAST][0]
STEP_WEIGHT = 0.5
VMEM_LIMIT = 61 * 1024 * 1024
BF = jnp.bfloat16
F32 = jnp.float32
I32 = jnp.int32
MESH = pl.DeviceIdType.MESH
NN = (((1,), (0,)), ((), ()))
NT = (((1,), (1,)), ((), ()))
TN = (((0,), (0,)), ((), ()))


def mm(a, b, dims):
    return lax.dot_general(a, b, dims, preferred_element_type=F32)


def iota(shape, dim):
    return lax.broadcasted_iota(I32, shape, dim)


def cos_sin(turns, period):
    rest = turns - jnp.floor(turns * (1.0 / period) + 0.5) * float(period)
    y = rest * (math.pi / period)
    z = y * y
    s = -1.0 / 39916800.0
    for term in (1.0 / 362880.0, -1.0 / 5040.0, 1.0 / 120.0, -1.0 / 6.0, 1.0):
        s = s * z + term
    s = s * y
    c = 1.0 / 479001600.0
    for term in (-1.0 / 3628800.0, 1.0 / 40320.0, -1.0 / 720.0, 1.0 / 24.0, -0.5, 1.0):
        c = c * z + term
    return 1.0 - 2.0 * s * s, 2.0 * s * c


def own_pairs(pair_v, me):
    mine = iota((ROUNDS, NW), 1) == me
    return jnp.sum(jnp.where(mine, pair_v[...], 0).astype(F32), axis=1, keepdims=True).astype(I32)


def rate_column(rates_v):
    diagonal = iota((LEV, LEV), 0) == iota((LEV, LEV), 1)
    return jnp.sum(jnp.where(diagonal, rates_v[...], 0.0), axis=1, keepdims=True)


def round_scalars(pair_mine, k):
    pair = pair_mine[k : k + 1, :]
    begin, length = PIECES[k]
    low = 2 * NW * k + pair
    high = 2 * NW * k + 2 * NW - 1 - pair
    split = begin + M - low
    even = pair % 2 == 0
    end = begin + length
    ranges = (
        jnp.where(even, begin, split),
        jnp.where(even, split, end),
        jnp.where(even, split, begin),
        jnp.where(even, end, split),
    )
    return low, high, split, ranges


def masked_basis(basis, ranges, k):
    a, b = WINDOWS[k]
    rows = a + iota((b - a, 1), 0)
    block = basis[a:b, :].astype(F32)
    even = (rows >= ranges[0]) & (rows < ranges[1])
    odd = (rows >= ranges[2]) & (rows < ranges[3])
    return jnp.concatenate(
        [jnp.where(even, block, 0.0).astype(BF), jnp.where(odd, block, 0.0).astype(BF)], axis=1
    )


def masked_across(flipped, ranges, k, shift):
    a, b = WINDOWS[k]
    rows = a + iota((1, b - a), 1)
    block = flipped[:, a - shift : b - shift].astype(F32)
    even = (rows >= ranges[0]) & (rows < ranges[1])
    odd = (rows >= ranges[2]) & (rows < ranges[3])
    return jnp.concatenate(
        [jnp.where(even, block, 0.0).astype(BF), jnp.where(odd, block, 0.0).astype(BF)], axis=0
    )


def make_picks(rows_v, pick):
    d = iota((NW, NW), 0)
    e = iota((NW, NW), 1)
    count_row = rows_v[...]
    before = e < d
    count = jnp.sum(jnp.where(e == d, count_row, 0).astype(F32), axis=1, keepdims=True)
    starts = jnp.sum(jnp.where(before, count_row, 0).astype(F32), axis=1, keepdims=True)
    single_rank = jnp.sum(jnp.where(before & (count_row == 1), 1.0, 0.0), axis=1, keepdims=True)
    lat = iota((NW, LAT), 1).astype(F32)
    hit = (starts <= lat) & (lat < starts + count)
    slot = jnp.sum(jnp.where(hit, lat - starts, 0.0), axis=0, keepdims=True)
    extra = jnp.where(slot >= 1.5, 1.0, 0.0)
    ahead = jnp.where(iota((LAT, LAT), 0) < iota((LAT, LAT), 1), 1.0, 0.0).astype(BF)
    extra8 = jnp.broadcast_to(extra, (16, LAT)).astype(BF)
    rank = mm(extra8, ahead, NN)[0:1, :]
    adopted = (extra > 0.5) & (rank == single_rank)
    second = jnp.where(count < 1.5, jnp.where(adopted, 1.0, 0.0), jnp.where(lat == starts + 1.0, 1.0, 0.0))
    pick[0:NW, :] = jnp.where(lat == starts, 1.0, 0.0).astype(BF)
    pick[NW : 2 * NW, :] = second.astype(BF)
    pick[2 * NW : 3 * NW, :] = jnp.where(lat == starts + 2.0, 1.0, 0.0).astype(BF)
    pick[3 * NW : 4 * NW, :] = jnp.where(lat == starts + 3.0, 1.0, 0.0).astype(BF)


def make_modes(lev, up, down):
    def fill(mode_index, level_index, same):
        phase = ((2 * level_index + 1) * mode_index).astype(F32)
        cosine, _ = cos_sin(phase, 4 * LEV)
        scale = jnp.where(mode_index == 0, math.sqrt(1.0 / LEV), math.sqrt(2.0 / LEV))
        return jnp.where(same, cosine * scale, 0.0).astype(BF)

    i, j = iota((128, 256), 0), iota((128, 256), 1)
    up[...] = fill(j % LEV, lev * LEVD + i % LEVD, i // LEVD == j // LEV)
    i, j = iota((256, 256), 0), iota((256, 256), 1)
    owner = jnp.where(j < 128, lev, 1 - lev)
    down[...] = fill(i % LEV, owner * LEVD + j % LEVD, i // LEV == (j // LEVD) % 2)


def make_spread(pair_mine, spread, start=0):
    for k in range(start, ROUNDS):
        a, b = WINDOWS[k]
        low, high, split, _ = round_scalars(pair_mine, k)
        rows = a + iota((1, b - a), 1)
        degree = jnp.where(rows < split, rows + (low - PIECES[k][0]), rows + (high - split)).astype(F32)
        value = degree * (degree + 1.0) / float(M * M)
        if k > start:
            width = 128
            first = jnp.where(rows[:, :width] < PIECES[k][0], spread[0:1, a : a + width], value[:, :width])
            spread[0:1, a : a + width] = first
            if b - a > width:
                spread[0:1, a + width : b] = value[:, width:]
        else:
            spread[0:1, a:b] = value


def make_table(pair_v, table):
    lane = iota((128, 128), 1).astype(F32)
    square = iota((NW, NW), 0) == iota((NW, NW), 1)
    for ch in range(CHUNKS):
        pairs = [
            jnp.sum(jnp.where(square, pair_v[k : k + 1, :], 0).astype(F32), axis=1, keepdims=True)
            for k in (2 * ch, 2 * ch + 1)
        ]
        pair = jnp.broadcast_to(jnp.concatenate(pairs, axis=0), (128, 128)).astype(I32)
        base = 2 * NW * (2 * ch + iota((128, 128), 0) // NW)
        low, high = base + pair, base + 2 * NW - 1 - pair
        even = pair % 2 == 0
        for par in range(2):
            wave = (jnp.where(even, low, high) if par == 0 else jnp.where(even, high, low)).astype(F32)
            c, s = cos_sin(wave * lane, NLON)
            c, s = c * NLON ** -0.5, s * NLON ** -0.5
            rc, rs = cos_sin(wave * 128.0, NLON)
            for b in range(TILES):
                lanes = slice(b * 128, (b + 1) * 128)
                if b == TILES - 1:
                    c, s = jnp.where(lane < HALF - 128.0 * b, c, 0.0), jnp.where(lane < HALF - 128.0 * b, s, 0.0)
                table[par, ch, 0:128, lanes] = c.astype(BF)
                table[par, ch, 128:256, lanes] = (-s).astype(BF)
                if b < TILES - 1:
                    c, s = c * rc - s * rs, s * rc + c * rs


def gather_spectra(sx, par):
    return jnp.concatenate(
        [
            jnp.concatenate(
                [
                    sx[pl.ds(kk * 8 + r * 4 + slot * 2 + par, NW, stride=16), :]
                    for r in range(2)
                    for kk in range(2)
                ],
                axis=0,
            )
            for slot in range(2)
        ],
        axis=1,
    ).astype(BF)


def synthesize(x, table, sx, acc, ch):
    sx[...] = x.astype(F32).reshape(NW * 16, 128)
    for par in range(2):
        part = mm(gather_spectra(sx, par), table[par, ch], TN)
        if ch == 0:
            acc[par] = part
        else:
            acc[par] = acc[par] + part


def slot_terms(acc, slot):
    base = slot * 128
    eu, ev = acc[0, base : base + 64, :], acc[0, base + 64 : base + 128, :]
    ou, ov = acc[1, base : base + 64, :], acc[1, base + 64 : base + 128, :]
    out = []
    for u, v in ((eu + ou, ev + ov), (eu - ou, ev - ov)):
        out.append(((-4.0 * u * v).astype(BF), (2.0 * (u * u - v * v)).astype(BF)))
    return out


def store_band(band, slot, f, first, second, keep):
    p = jnp.where(keep, first.astype(F32), 0.0)
    q = jnp.where(keep, second.astype(F32), 0.0)
    rolled = pltpu.roll(q, 64, axis=1)
    band[slot, f, :, 0:1280] = p[:, 0:1280].astype(BF)
    band[slot, f, :, 1280:1408] = (p[:, 1280:1408] + rolled[:, 0:128]).astype(BF)
    band[slot, f, :, 1408:2688] = rolled[:, 128:1408].astype(BF)


def direct_chunk(own, across, ch, pair_mine, flipped, shift, spread, rates, pick, down, up, state, sx, sy):
    sx[...] = own.astype(F32).reshape(NW * 16, 128)
    sy[...] = across.astype(F32).reshape(NW * 16, 128)
    for kk in range(2):
        k = 2 * ch + kk
        a, b = WINDOWS[k]
        _, _, _, ranges = round_scalars(pair_mine, k)
        both = masked_across(flipped, ranges, k, shift)
        factor = STEP_WEIGHT / (1.0 + rates[...] * spread[0:1, a:b])
        factor = jnp.concatenate([factor, factor], axis=0)
        for r in range(2):
            weighted = []
            for par in range(2):
                at = [kk * 8 + r * 4 + slot * 2 + par for slot in range(2)]
                gathered = jnp.concatenate(
                    [jnp.concatenate([s[pl.ds(i, NW, stride=16), :] for i in at], axis=0) for s in (sx, sy)],
                    axis=1,
                ).astype(BF)
                by_lat = mm(pick[0 : 2 * NW, :], gathered, TN).astype(BF)
                weighted.append(mm(by_lat, down[...], NT).astype(BF))
            pair = jnp.concatenate(weighted, axis=0)
            modes = (mm(pair, both, TN) * factor).astype(BF)
            change = mm(up[...], modes, NN)
            for f in range(2):
                c = 2 * f + r
                at = slice(a - shift, b - shift)
                state[c, :, at] = (state[c, :, at].astype(F32) + change[f * 64 : (f + 1) * 64]).astype(BF)


def finish(
    pair_v, rows_v, rates_v, new_in, band_in, own_in, across_in, flip_in,
    new_out, band_out,
    state, tail, band, own, across, flipped, sx, sy, pick, up, down, spread, rates, load_sem, save_sem,
):
    me = lax.axis_index("wave")
    lev = lax.axis_index("lev")
    ends = (pl.ds(0, 4), pl.ds(0, LEVD), pl.ds(TAIL, NR - TAIL))
    width = TAIL // 3
    parts = [(pl.ds(0, 4), pl.ds(0, LEVD), pl.ds(i * width, width)) for i in range(3)]
    halves = [pl.ds(0, 2), pl.ds(2, 2)]
    loads = [(new_in.at[at], state.at[at], new_out.at[at]) for at in parts]
    loads += [(band_in.at[at], band.at[at], band_out.at[at]) for at in halves]
    through = [pltpu.make_async_copy(a, b, load_sem.at[i]) for i, (a, b, _) in enumerate(loads)]
    away = [pltpu.make_async_copy(b, c, save_sem.at[i]) for i, (_, b, c) in enumerate(loads)]
    needed = [
        pltpu.make_async_copy(a, b, load_sem.at[len(loads) + i])
        for i, (a, b) in enumerate(
            ((own_in, own), (across_in, across), (flip_in, flipped), (new_in.at[ends], tail))
        )
    ]
    for copy in through + needed:
        copy.start()
    pair_mine = own_pairs(pair_v, me)
    make_picks(rows_v, pick)
    make_modes(lev, up, down)
    make_spread(pair_mine, spread, 2 * LAST)
    rates[...] = rate_column(rates_v)
    for load, save in zip(through, away):
        load.wait()
        save.start()
    for copy in needed:
        copy.wait()
    for ch in range(LAST, CHUNKS):
        direct_chunk(
            own[ch - LAST], across[ch - LAST], ch, pair_mine, flipped, TAIL, spread, rates, pick, down, up, tail, sx, sy
        )
    rest = pltpu.make_async_copy(tail, new_out.at[ends], save_sem.at[len(loads)])
    rest.start()
    for copy in away:
        copy.wait()
    rest.wait()


def body(
    pair_v, rows_v, weights_v, rates_v, state_in, basis_in,
    new_out, band_out, own_out, across_out, flip_out,
    state, basis, flipped, band, other, table, st_a, st_b, st_c, rv_a, rv_b, rv_c, rv_p, sx, sy, acc, tp,
    pick, up, down, spread, rates,
    send_sem, ra_sem, rb_sem, rc_sem, rp_sem, state_sem, own_sem, io_sem,
):
    me = lax.axis_index("wave")
    lev = lax.axis_index("lev")
    z, y, x = me // 16, (me // 4) % 4, me % 4
    across = 1 - lev

    load_state = pltpu.make_async_copy(state_in, state, io_sem.at[0])
    load_basis = pltpu.make_async_copy(basis_in, basis, io_sem.at[1])
    load_state.start()
    load_basis.start()

    across_x = [(x + d) % 4 for d in range(4)]

    def each_peer(action):
        def peer(i, d):
            return (z + i // 4 + d + i % 4) % 4 * 16 + (y + i % 4 + d) % 4 * 4 + across_x[d]

        for d in range(1, 4):
            action(peer(0, d))

        def step(i, carry):
            for d in range(4):
                action(peer(i, d))
            return carry

        lax.fori_loop(1, 16, step, 0)

    barrier = pltpu.get_barrier_semaphore()
    each_peer(lambda p: pl.semaphore_signal(barrier, inc=1, device_id={"wave": p}, device_id_type=MESH))
    pl.semaphore_signal(barrier, inc=1, device_id={"lev": across}, device_id_type=MESH)

    pair_mine = own_pairs(pair_v, me)
    make_picks(rows_v, pick)
    make_modes(lev, up, down)
    make_spread(pair_mine, spread)
    diagonal = iota((LEV, LEV), 0) == iota((LEV, LEV), 1)
    rates[...] = rate_column(rates_v)
    rows_mine = jnp.sum(
        jnp.where(iota((1, NW), 1) == me, rows_v[...], 0).astype(F32), axis=1, keepdims=True
    )

    pl.semaphore_wait(barrier, NW)
    swap = pltpu.make_async_remote_copy(
        src_ref=state_in, dst_ref=other, send_sem=state_sem.at[0], recv_sem=state_sem.at[1],
        device_id={"lev": across}, device_id_type=MESH,
    )

    def own(stage, land, which, g, group):
        at = pl.ds(group[0], group[1])
        return pltpu.make_async_copy(stage.at[at, me], land.at[at, me], own_sem.at[which, g])

    def send(stage, land, sems, which, g, group):
        at = pl.ds(group[0], group[1])
        own(stage, land, which, g, group).start()

        def one(p):
            pltpu.make_async_remote_copy(
                src_ref=stage.at[at, p], dst_ref=land.at[at, me], send_sem=send_sem.at[which, g],
                recv_sem=sems.at[g], device_id={"wave": p}, device_id_type=MESH,
            ).start()

        each_peer(one)

    def many(stage, land, sems, which, g, group):
        at = (pl.ds(group[0], group[1]), pl.ds(0, NW - 1))
        return pltpu.make_async_remote_copy(
            src_ref=stage.at[at], dst_ref=land.at[at],
            send_sem=send_sem.at[which, g], recv_sem=sems.at[g], device_id={"wave": me}, device_id_type=MESH,
        )

    def arrive(stage, land, sems, which, g, group):
        own(stage, land, which, g, group).wait()
        many(stage, land, sems, which, g, group).wait_recv()

    load_basis.wait()
    load_state.wait()
    for g, group in enumerate(GROUPS):
        for ch in range(group[0], sum(group)):
            for kk in range(2):
                k = 2 * ch + kk
                a, b = WINDOWS[k]
                low, _, _, ranges = round_scalars(pair_mine, k)
                both = masked_basis(basis, ranges, k)
                rows = jnp.concatenate([state[c, :, a:b] for c in (0, 2, 1, 3)], axis=0)
                product = mm(rows, both, NN)
                for par in range(2):
                    part = product[:, par * LAT : (par + 1) * LAT]
                    if k == 0 and par == 0:
                        part = part * jnp.where(low == 0, 0.5, 1.0)
                    picked = mm(pick[...], part.astype(BF), NT)
                    for r in range(2):
                        lanes = slice(r * 128, (r + 1) * 128)
                        for slot in range(2):
                            at = kk * 8 + r * 4 + slot * 2 + par
                            sx[pl.ds(at, NW, stride=16), :] = picked[slot * NW : (slot + 1) * NW, lanes]
                            sy[pl.ds(at, NW, stride=16), :] = picked[(2 + slot) * NW : (3 + slot) * NW, lanes]
            st_a[ch] = sx[...].reshape(NW, 16, 128).astype(BF)
            st_b[ch] = sy[...].reshape(NW, 16, 128).astype(BF)
        send(st_a, rv_a, ra_sem, 0, g, group)
        if g == 0:
            swap.start()

    send(st_b, rv_b, rb_sem, 1, 0, EXTRA[0])

    make_table(pair_v, table)
    tile = HPAD
    unit = jnp.where(diagonal, 1.0, 0.0).astype(BF)
    for a in range(0, NR, tile):
        b = min(a + tile, NR)
        flipped[:, a:b] = mm(unit, basis[a:b, :], NT).astype(BF)

    save_flip = pltpu.make_async_copy(
        flipped.at[pl.ds(0, LAT), pl.ds(TAIL, NR - TAIL)], flip_out, io_sem.at[6 + len(GROUPS)]
    )
    save_flip.start()

    def couple(first, last):
        for a in range(first * tile, min(last * tile, NR), tile):
            b = min(a + tile, NR)
            factor = 1.0 / (1.0 + rates[...] * spread[0:1, a:b])
            factor = jnp.concatenate([factor, factor], axis=0)
            for r in range(2):
                levels = jnp.concatenate(
                    [state[r, :, a:b], state[2 + r, :, a:b], other[r, :, a:b], other[2 + r, :, a:b]], axis=0
                )
                modes = (mm(down[...], levels, NN) * factor).astype(BF)
                result = mm(up[...], modes, NN).astype(BF)
                state[r, :, a:b] = result[0:64]
                state[2 + r, :, a:b] = result[64:128]

    swap.wait_recv()
    couple(0, 5)

    for g, group in enumerate(GROUPS):
        arrive(st_a, rv_a, ra_sem, 0, g, group)
        for ch in range(group[0], sum(group)):
            synthesize(rv_a[ch], table, sx, acc, ch)

    for slot in range(2):
        first, second = slot_terms(acc, slot)
        for f in range(2):
            at = slot * 128 + f * 64
            p, q = first[f].astype(F32), second[f].astype(F32)
            tp[0, at : at + 64, :] = (p + q).astype(BF)
            tp[1, at : at + 64, :] = (p - q).astype(BF)
            store_band(band, slot, f, first[f], second[f], rows_mine > slot + 0.5)
    save_home = pltpu.make_async_copy(band.at[pl.ds(0, 2)], band_out.at[pl.ds(0, 2)], io_sem.at[2])
    save_extra = pltpu.make_async_copy(band.at[pl.ds(2, 2)], band_out.at[pl.ds(2, 2)], io_sem.at[3])
    save_home.start()

    slot_row = iota((2 * NW, LAT), 0)
    weight = [
        jnp.sum(
            jnp.where(slot_row == slot * NW + me, pick[0 : 2 * NW, :].astype(F32) * weights_v[...], 0.0),
            axis=(0, 1), keepdims=True,
        )
        for slot in range(2)
    ]
    for g, group in enumerate(GROUPS):
        for ch in range(group[0], sum(group)):
            for par in range(2):
                coeff = mm(table[par, ch], tp[par], NT).astype(BF).astype(F32)
                for slot in range(2):
                    part = coeff[:, slot * 128 : (slot + 1) * 128] * weight[slot]
                    for r in range(2):
                        for kk in range(2):
                            at = r * 128 + kk * NW
                            sx[pl.ds(kk * 8 + r * 4 + slot * 2 + par, NW, stride=16), :] = part[at : at + NW]
            st_c[ch] = sx[...].reshape(NW, 16, 128).astype(BF)
        send(st_c, rv_c, rc_sem, 2, g, group)

    couple(5, 10)

    arrive(st_b, rv_b, rb_sem, 1, 0, EXTRA[0])
    for ch in range(CHUNKS):
        synthesize(rv_b[ch], table, sx, acc, ch)
    for slot in range(2):
        first, second = slot_terms(acc, slot)
        for f in range(2):
            store_band(band, 2 + slot, f, first[f], second[f], rows_mine > slot + 2.5)
    save_extra.start()

    def forward(g, group):
        at = pl.ds(group[0], group[1])
        return pltpu.make_async_remote_copy(
            src_ref=rv_c.at[at], dst_ref=rv_p.at[at], send_sem=send_sem.at[3, g], recv_sem=rp_sem.at[g],
            device_id={"lev": across}, device_id_type=MESH,
        )

    saves = []

    def save(stop, g):
        a = WINDOWS[2 * GROUPS[g][0]][0]
        at = (pl.ds(0, 4), pl.ds(0, LEVD), pl.ds(a, stop - a))
        copy = pltpu.make_async_copy(state.at[at], new_out.at[at], io_sem.at[4 + g])
        copy.start()
        saves.append(copy)

    def direct(g, group):
        forward(g, group).wait_recv()
        for ch in range(group[0], sum(group)):
            direct_chunk(
                rv_c[ch], rv_p[ch], ch, pair_mine, flipped, 0, spread, rates, pick, down, up, state, sx, sy
            )
        save(WINDOWS[2 * sum(group)][0], g)

    for g, group in enumerate(GROUPS):
        arrive(st_c, rv_c, rc_sem, 2, g, group)
        forward(g, group).start()
        if g > 0:
            direct(g - 1, GROUPS[g - 1])
    save(NR, len(GROUPS) - 1)
    forward(len(GROUPS) - 1, GROUPS[-1]).wait_recv()
    last = pl.ds(LAST, CHUNKS - LAST)
    for i, (ref, out) in enumerate(((rv_c, own_out), (rv_p, across_out))):
        copy = pltpu.make_async_copy(ref.at[last], out, io_sem.at[4 + len(GROUPS) + i])
        copy.start()
        saves.append(copy)
    saves.append(save_flip)

    swap.wait_send()
    for g, group in enumerate(GROUPS):
        many(st_a, rv_a, ra_sem, 0, g, group).wait_send()
        many(st_c, rv_c, rc_sem, 2, g, group).wait_send()
        forward(g, group).wait_send()
    many(st_b, rv_b, rb_sem, 1, 0, EXTRA[0]).wait_send()
    save_home.wait()
    save_extra.wait()
    for copy in saves:
        copy.wait()


def local(spectral_state, legendre_basis, pairing, band_rows, weights, mode_rates):
    vmem = pl.BlockSpec(memory_space=pltpu.VMEM)
    anywhere = pl.BlockSpec(memory_space=pl.ANY)
    stage = pltpu.VMEM((CHUNKS, NW, 16, 128), BF)
    work = pltpu.VMEM((NW * 16, 128), F32)
    sems = pltpu.SemaphoreType.DMA((len(GROUPS),))
    results = (
        jax.ShapeDtypeStruct((4, LEVD, NR), BF),
        jax.ShapeDtypeStruct((4, 2, LEVD, NLON), BF),
    )
    part = (CHUNKS - LAST, NW, 16, 128)
    handed = results + (
        jax.ShapeDtypeStruct(part, BF),
        jax.ShapeDtypeStruct(part, BF),
        jax.ShapeDtypeStruct((LAT, NR - TAIL), BF),
    )
    constants = [
        pltpu.VMEM((256, 128), BF),
        pltpu.VMEM((128, 256), BF),
        pltpu.VMEM((256, 256), BF),
        pltpu.VMEM((8, NR), F32),
        pltpu.VMEM((LEV, 1), F32),
    ]
    pairs, rows, rates = pairing.T, band_rows[None, :], mode_rates[None, :]
    passed = pl.pallas_call(
        body,
        out_shape=handed,
        in_specs=[vmem] * 4 + [anywhere] * 2,
        out_specs=(anywhere,) * 5,
        scratch_shapes=[
            pltpu.VMEM((4, LEVD, NR), BF),
            pltpu.VMEM((NR, LAT), BF),
            pltpu.VMEM((LAT, NR), BF),
            pltpu.VMEM((4, 2, LEVD, NLON), BF),
            pltpu.VMEM((4, LEVD, NR), BF),
            pltpu.VMEM((2, CHUNKS, 256, HPAD), BF),
            stage, stage, stage, stage, stage, stage, stage,
            work, work,
            pltpu.VMEM((2, 256, HPAD), F32),
            pltpu.VMEM((2, 256, HPAD), BF),
            *constants,
            pltpu.SemaphoreType.DMA((4, len(GROUPS))),
            sems, sems, sems, sems,
            pltpu.SemaphoreType.DMA((2,)),
            pltpu.SemaphoreType.DMA((3, len(GROUPS))),
            pltpu.SemaphoreType.DMA((7 + len(GROUPS),)),
        ],
        compiler_params=pltpu.CompilerParams(
            collective_id=0, has_side_effects=True, vmem_limit_bytes=VMEM_LIMIT
        ),
    )(pairs, rows, weights[None, :], rates, spectral_state, legendre_basis)
    return pl.pallas_call(
        finish,
        out_shape=results,
        in_specs=[vmem] * 3 + [anywhere] * 5,
        out_specs=(anywhere, anywhere),
        scratch_shapes=[
            pltpu.VMEM((4, LEVD, TAIL), BF),
            pltpu.VMEM((4, LEVD, NR - TAIL), BF),
            pltpu.VMEM((4, 2, LEVD, NLON), BF),
            pltpu.VMEM(part, BF),
            pltpu.VMEM(part, BF),
            pltpu.VMEM((LAT, NR - TAIL), BF),
            work, work,
            *constants,
            pltpu.SemaphoreType.DMA((9,)),
            pltpu.SemaphoreType.DMA((6,)),
        ],
        compiler_params=pltpu.CompilerParams(vmem_limit_bytes=VMEM_LIMIT),
    )(pairs, rows, rates, *passed)


def solution(mesh):
    in_specs = (P(None, "lev", "wave"), P("wave", None), P(), P(), P(), P())
    out_specs = (P(None, "lev", "wave"), P("wave", None, "lev", None))
    return jax.shard_map(local, mesh=mesh, in_specs=in_specs, out_specs=out_specs, check_vma=False)
```

```python
import functools
import math

import jax
import jax.numpy as jnp
from jax import lax
from jax.experimental import pallas as pl
from jax.experimental.pallas import tpu as pltpu
from jax.sharding import PartitionSpec as P

M = 1280
NLON = 2688
HALF = NLON // 2
TILES = 11
HPAD = 128 * TILES
LAT = 128
NW = 64
NR = 12810
LEV = 128
LEVD = 64
ROUNDS = M // (2 * NW)
CHUNKS = ROUNDS // 2
PIECES = []
_offset = 0
for _k in range(ROUNDS):
    _length = 2 * M - 4 * _k * NW - 2 * NW + 1
    PIECES.append((_offset, _length))
    _offset += _length
GROUPS = ((0, 1), (1, 2), (3, 1), (4, 1))
FIRST = ((3, 2), (1, 2), (0, 1))
EXTRA = ((0, CHUNKS),)
LAST = GROUPS[-1][0]
WINDOWS = [(o // 128 * 128, min(-(-(o + n) // 128) * 128, NR)) for o, n in PIECES]
TAIL = WINDOWS[2 * LAST][0]
STEP_WEIGHT = 0.5
VMEM_LIMIT = 61 * 1024 * 1024
BF = jnp.bfloat16
F32 = jnp.float32
I32 = jnp.int32
MESH = pl.DeviceIdType.MESH
NN = (((1,), (0,)), ((), ()))
NT = (((1,), (1,)), ((), ()))
TN = (((0,), (0,)), ((), ()))


def mm(a, b, dims):
    return lax.dot_general(a, b, dims, preferred_element_type=F32)


def iota(shape, dim):
    return lax.broadcasted_iota(I32, shape, dim)


def cos_sin(turns, period):
    rest = turns - jnp.floor(turns * (1.0 / period) + 0.5) * float(period)
    y = rest * (math.pi / period)
    z = y * y
    s = -1.0 / 39916800.0
    for term in (1.0 / 362880.0, -1.0 / 5040.0, 1.0 / 120.0, -1.0 / 6.0, 1.0):
        s = s * z + term
    s = s * y
    c = 1.0 / 479001600.0
    for term in (-1.0 / 3628800.0, 1.0 / 40320.0, -1.0 / 720.0, 1.0 / 24.0, -0.5, 1.0):
        c = c * z + term
    return 1.0 - 2.0 * s * s, 2.0 * s * c


def own_pairs(pair_v, me):
    mine = iota((ROUNDS, NW), 1) == me
    return jnp.sum(jnp.where(mine, pair_v[...], 0).astype(F32), axis=1, keepdims=True).astype(I32)


def rate_column(rates_v):
    diagonal = iota((LEV, LEV), 0) == iota((LEV, LEV), 1)
    return jnp.sum(jnp.where(diagonal, rates_v[...], 0.0), axis=1, keepdims=True)


def round_scalars(pair_mine, k):
    pair = pair_mine[k : k + 1, :]
    begin, length = PIECES[k]
    low = 2 * NW * k + pair
    high = 2 * NW * k + 2 * NW - 1 - pair
    split = begin + M - low
    even = pair % 2 == 0
    end = begin + length
    ranges = (
        jnp.where(even, begin, split),
        jnp.where(even, split, end),
        jnp.where(even, split, begin),
        jnp.where(even, end, split),
    )
    return low, high, split, ranges


def masked_basis(basis, ranges, k):
    a, b = WINDOWS[k]
    rows = a + iota((b - a, 1), 0)
    block = basis[a:b, :].astype(F32)
    even = (rows >= ranges[0]) & (rows < ranges[1])
    odd = (rows >= ranges[2]) & (rows < ranges[3])
    return jnp.concatenate(
        [jnp.where(even, block, 0.0).astype(BF), jnp.where(odd, block, 0.0).astype(BF)], axis=1
    )


def masked_across(flipped, ranges, k, shift):
    a, b = WINDOWS[k]
    rows = a + iota((1, b - a), 1)
    block = flipped[:, a - shift : b - shift].astype(F32)
    even = (rows >= ranges[0]) & (rows < ranges[1])
    odd = (rows >= ranges[2]) & (rows < ranges[3])
    return jnp.concatenate(
        [jnp.where(even, block, 0.0).astype(BF), jnp.where(odd, block, 0.0).astype(BF)], axis=0
    )


def make_picks(rows_v, pick):
    d = iota((NW, NW), 0)
    e = iota((NW, NW), 1)
    count_row = rows_v[...]
    before = e < d
    count = jnp.sum(jnp.where(e == d, count_row, 0).astype(F32), axis=1, keepdims=True)
    starts = jnp.sum(jnp.where(before, count_row, 0).astype(F32), axis=1, keepdims=True)
    single_rank = jnp.sum(jnp.where(before & (count_row == 1), 1.0, 0.0), axis=1, keepdims=True)
    lat = iota((NW, LAT), 1).astype(F32)
    hit = (starts <= lat) & (lat < starts + count)
    slot = jnp.sum(jnp.where(hit, lat - starts, 0.0), axis=0, keepdims=True)
    extra = jnp.where(slot >= 1.5, 1.0, 0.0)
    ahead = jnp.where(iota((LAT, LAT), 0) < iota((LAT, LAT), 1), 1.0, 0.0).astype(BF)
    extra8 = jnp.broadcast_to(extra, (16, LAT)).astype(BF)
    rank = mm(extra8, ahead, NN)[0:1, :]
    adopted = (extra > 0.5) & (rank == single_rank)
    second = jnp.where(count < 1.5, jnp.where(adopted, 1.0, 0.0), jnp.where(lat == starts + 1.0, 1.0, 0.0))
    pick[0:NW, :] = jnp.where(lat == starts, 1.0, 0.0).astype(BF)
    pick[NW : 2 * NW, :] = second.astype(BF)
    pick[2 * NW : 3 * NW, :] = jnp.where(lat == starts + 2.0, 1.0, 0.0).astype(BF)
    pick[3 * NW : 4 * NW, :] = jnp.where(lat == starts + 3.0, 1.0, 0.0).astype(BF)


def make_modes(lev, up, down):
    def fill(mode_index, level_index, same):
        phase = ((2 * level_index + 1) * mode_index).astype(F32)
        cosine, _ = cos_sin(phase, 4 * LEV)
        scale = jnp.where(mode_index == 0, math.sqrt(1.0 / LEV), math.sqrt(2.0 / LEV))
        return jnp.where(same, cosine * scale, 0.0).astype(BF)

    i, j = iota((128, 256), 0), iota((128, 256), 1)
    up[...] = fill(j % LEV, lev * LEVD + i % LEVD, i // LEVD == j // LEV)
    i, j = iota((256, 256), 0), iota((256, 256), 1)
    owner = jnp.where(j < 128, lev, 1 - lev)
    down[...] = fill(i % LEV, owner * LEVD + j % LEVD, i // LEV == (j // LEVD) % 2)


def make_spread(pair_mine, spread, start=0):
    for k in range(start, ROUNDS):
        a, b = WINDOWS[k]
        low, high, split, _ = round_scalars(pair_mine, k)
        rows = a + iota((1, b - a), 1)
        degree = jnp.where(rows < split, rows + (low - PIECES[k][0]), rows + (high - split)).astype(F32)
        value = degree * (degree + 1.0) / float(M * M)
        if k > start:
            width = 128
            first = jnp.where(rows[:, :width] < PIECES[k][0], spread[0:1, a : a + width], value[:, :width])
            spread[0:1, a : a + width] = first
            if b - a > width:
                spread[0:1, a + width : b] = value[:, width:]
        else:
            spread[0:1, a:b] = value


def make_table(pair_v, table):
    lane = iota((128, 128), 1).astype(F32)
    square = iota((NW, NW), 0) == iota((NW, NW), 1)
    for ch in range(CHUNKS):
        pairs = [
            jnp.sum(jnp.where(square, pair_v[k : k + 1, :], 0).astype(F32), axis=1, keepdims=True)
            for k in (2 * ch, 2 * ch + 1)
        ]
        pair = jnp.broadcast_to(jnp.concatenate(pairs, axis=0), (128, 128)).astype(I32)
        base = 2 * NW * (2 * ch + iota((128, 128), 0) // NW)
        low, high = base + pair, base + 2 * NW - 1 - pair
        even = pair % 2 == 0
        for par in range(2):
            wave = (jnp.where(even, low, high) if par == 0 else jnp.where(even, high, low)).astype(F32)
            c, s = cos_sin(wave * lane, NLON)
            c, s = c * NLON ** -0.5, s * NLON ** -0.5
            rc, rs = cos_sin(wave * 128.0, NLON)
            for b in range(TILES):
                lanes = slice(b * 128, (b + 1) * 128)
                if b == TILES - 1:
                    c, s = jnp.where(lane < HALF - 128.0 * b, c, 0.0), jnp.where(lane < HALF - 128.0 * b, s, 0.0)
                table[par, ch, 0:128, lanes] = c.astype(BF)
                table[par, ch, 128:256, lanes] = (-s).astype(BF)
                if b < TILES - 1:
                    c, s = c * rc - s * rs, s * rc + c * rs


def gather_spectra(sx, par):
    return jnp.concatenate(
        [
            jnp.concatenate(
                [
                    sx[pl.ds(kk * 8 + r * 4 + slot * 2 + par, NW, stride=16), :]
                    for r in range(2)
                    for kk in range(2)
                ],
                axis=0,
            )
            for slot in range(2)
        ],
        axis=1,
    ).astype(BF)


def synthesize(x, table, sx, acc, ch, first):
    sx[...] = x.astype(F32).reshape(NW * 16, 128)
    for par in range(2):
        part = mm(gather_spectra(sx, par), table[par, ch], TN)
        if first:
            acc[par] = part
        else:
            acc[par] = acc[par] + part


def slot_terms(acc, slot):
    base = slot * 128
    eu, ev = acc[0, base : base + 64, :], acc[0, base + 64 : base + 128, :]
    ou, ov = acc[1, base : base + 64, :], acc[1, base + 64 : base + 128, :]
    out = []
    for u, v in ((eu + ou, ev + ov), (eu - ou, ev - ov)):
        out.append(((-4.0 * u * v).astype(BF), (2.0 * (u * u - v * v)).astype(BF)))
    return out


def store_band(band, slot, f, first, second, keep):
    p = jnp.where(keep, first.astype(F32), 0.0)
    q = jnp.where(keep, second.astype(F32), 0.0)
    rolled = pltpu.roll(q, 64, axis=1)
    band[slot, f, :, 0:1280] = p[:, 0:1280].astype(BF)
    band[slot, f, :, 1280:1408] = (p[:, 1280:1408] + rolled[:, 0:128]).astype(BF)
    band[slot, f, :, 1408:2688] = rolled[:, 128:1408].astype(BF)


def direct_chunk(own, across, ch, pair_mine, flipped, shift, spread, rates, pick, down, up, state, sx, sy, between=None):
    sx[...] = own.astype(F32).reshape(NW * 16, 128)
    sy[...] = across.astype(F32).reshape(NW * 16, 128)
    for kk in range(2):
        if kk == 1 and between is not None:
            between()
        k = 2 * ch + kk
        a, b = WINDOWS[k]
        _, _, _, ranges = round_scalars(pair_mine, k)
        both = masked_across(flipped, ranges, k, shift)
        factor = STEP_WEIGHT / (1.0 + rates[...] * spread[0:1, a:b])
        factor = jnp.concatenate([factor, factor], axis=0)
        for r in range(2):
            weighted = []
            for par in range(2):
                at = [kk * 8 + r * 4 + slot * 2 + par for slot in range(2)]
                gathered = jnp.concatenate(
                    [jnp.concatenate([s[pl.ds(i, NW, stride=16), :] for i in at], axis=0) for s in (sx, sy)],
                    axis=1,
                ).astype(BF)
                by_lat = mm(pick[0 : 2 * NW, :], gathered, TN).astype(BF)
                weighted.append(mm(by_lat, down[...], NT).astype(BF))
            pair = jnp.concatenate(weighted, axis=0)
            modes = (mm(pair, both, TN) * factor).astype(BF)
            change = mm(up[...], modes, NN)
            for f in range(2):
                c = 2 * f + r
                at = slice(a - shift, b - shift)
                state[c, :, at] = (state[c, :, at].astype(F32) + change[f * 64 : (f + 1) * 64]).astype(BF)


def finish(
    pair_v, rows_v, rates_v, new_in, band_in, own_in, across_in, flip_in,
    new_out, band_out,
    state, tail, band, own, across, flipped, sx, sy, pick, up, down, spread, rates, load_sem, save_sem,
):
    me = lax.axis_index("wave")
    lev = lax.axis_index("lev")
    ends = (pl.ds(0, 4), pl.ds(0, LEVD), pl.ds(TAIL, NR - TAIL))
    width = TAIL // 3
    parts = [(pl.ds(0, 4), pl.ds(0, LEVD), pl.ds(i * width, width)) for i in range(3)]
    halves = [pl.ds(0, 2), pl.ds(2, 2)]
    loads = [(new_in.at[at], state.at[at], new_out.at[at]) for at in parts]
    loads += [(band_in.at[at], band.at[at], band_out.at[at]) for at in halves]
    through = [pltpu.make_async_copy(a, b, load_sem.at[i]) for i, (a, b, _) in enumerate(loads)]
    away = [pltpu.make_async_copy(b, c, save_sem.at[i]) for i, (_, b, c) in enumerate(loads)]
    needed = [
        pltpu.make_async_copy(a, b, load_sem.at[len(loads) + i])
        for i, (a, b) in enumerate(
            ((own_in, own), (across_in, across), (flip_in, flipped), (new_in.at[ends], tail))
        )
    ]
    for copy in needed + through:
        copy.start()
    pair_mine = own_pairs(pair_v, me)
    make_picks(rows_v, pick)
    make_modes(lev, up, down)
    make_spread(pair_mine, spread, 2 * LAST)
    rates[...] = rate_column(rates_v)
    def move(first, last):
        for load, save in zip(through[first:last], away[first:last]):
            load.wait()
            save.start()

    for copy in needed:
        copy.wait()
    for ch in range(LAST, CHUNKS):
        direct_chunk(
            own[ch - LAST], across[ch - LAST], ch, pair_mine, flipped, TAIL, spread, rates, pick, down, up, tail, sx, sy,
            functools.partial(move, 0, 2),
        )
    move(2, 5)
    rest = pltpu.make_async_copy(tail, new_out.at[ends], save_sem.at[len(loads)])
    rest.start()
    for copy in away:
        copy.wait()
    rest.wait()


def body(
    pair_v, rows_v, weights_v, rates_v, state_in, basis_in,
    new_out, band_out, own_out, across_out, flip_out,
    state, basis, flipped, band, other, table, st_a, st_b, st_c, rv_a, rv_b, rv_c, rv_p, sx, sy, acc, tp,
    pick, up, down, spread, rates,
    send_sem, ra_sem, rb_sem, rc_sem, rp_sem, state_sem, own_sem, io_sem,
):
    me = lax.axis_index("wave")
    lev = lax.axis_index("lev")
    z, y, x = me // 16, (me // 4) % 4, me % 4
    across = 1 - lev

    load_state = pltpu.make_async_copy(state_in, state, io_sem.at[0])
    load_basis = pltpu.make_async_copy(basis_in, basis, io_sem.at[1])
    load_state.start()
    load_basis.start()

    across_x = [(x + d) % 4 for d in range(4)]

    def each_peer(action):
        def peer(i, d):
            return (z + i // 4 + d + i % 4) % 4 * 16 + (y + i % 4 + d) % 4 * 4 + across_x[d]

        for d in range(1, 4):
            action(peer(0, d))

        def step(i, carry):
            for d in range(4):
                action(peer(i, d))
            return carry

        lax.fori_loop(1, 16, step, 0)

    barrier = pltpu.get_barrier_semaphore()
    each_peer(lambda p: pl.semaphore_signal(barrier, inc=1, device_id={"wave": p}, device_id_type=MESH))
    pl.semaphore_signal(barrier, inc=1, device_id={"lev": across}, device_id_type=MESH)

    pair_mine = own_pairs(pair_v, me)
    make_picks(rows_v, pick)
    make_modes(lev, up, down)
    make_spread(pair_mine, spread)
    diagonal = iota((LEV, LEV), 0) == iota((LEV, LEV), 1)
    rates[...] = rate_column(rates_v)
    rows_mine = jnp.sum(
        jnp.where(iota((1, NW), 1) == me, rows_v[...], 0).astype(F32), axis=1, keepdims=True
    )

    pl.semaphore_wait(barrier, NW)
    swap = pltpu.make_async_remote_copy(
        src_ref=state_in, dst_ref=other, send_sem=state_sem.at[0], recv_sem=state_sem.at[1],
        device_id={"lev": across}, device_id_type=MESH,
    )

    def own(stage, land, which, g, group):
        at = pl.ds(group[0], group[1])
        return pltpu.make_async_copy(stage.at[at, me], land.at[at, me], own_sem.at[which, g])

    def send(stage, land, sems, which, g, group):
        at = pl.ds(group[0], group[1])
        own(stage, land, which, g, group).start()

        def one(p):
            pltpu.make_async_remote_copy(
                src_ref=stage.at[at, p], dst_ref=land.at[at, me], send_sem=send_sem.at[which, g],
                recv_sem=sems.at[g], device_id={"wave": p}, device_id_type=MESH,
            ).start()

        each_peer(one)

    def many(stage, land, sems, which, g, group):
        at = (pl.ds(group[0], group[1]), pl.ds(0, NW - 1))
        return pltpu.make_async_remote_copy(
            src_ref=stage.at[at], dst_ref=land.at[at],
            send_sem=send_sem.at[which, g], recv_sem=sems.at[g], device_id={"wave": me}, device_id_type=MESH,
        )

    def arrive(stage, land, sems, which, g, group):
        own(stage, land, which, g, group).wait()
        many(stage, land, sems, which, g, group).wait_recv()

    load_basis.wait()
    load_state.wait()
    for g, group in enumerate(FIRST):
        for ch in range(group[0], sum(group)):
            for kk in range(2):
                k = 2 * ch + kk
                a, b = WINDOWS[k]
                low, _, _, ranges = round_scalars(pair_mine, k)
                both = masked_basis(basis, ranges, k)
                rows = jnp.concatenate([state[c, :, a:b] for c in (0, 2, 1, 3)], axis=0)
                product = mm(rows, both, NN)
                for par in range(2):
                    part = product[:, par * LAT : (par + 1) * LAT]
                    if k == 0 and par == 0:
                        part = part * jnp.where(low == 0, 0.5, 1.0)
                    picked = mm(pick[...], part.astype(BF), NT)
                    for r in range(2):
                        lanes = slice(r * 128, (r + 1) * 128)
                        for slot in range(2):
                            at = kk * 8 + r * 4 + slot * 2 + par
                            sx[pl.ds(at, NW, stride=16), :] = picked[slot * NW : (slot + 1) * NW, lanes]
                            sy[pl.ds(at, NW, stride=16), :] = picked[(2 + slot) * NW : (3 + slot) * NW, lanes]
            st_a[ch] = sx[...].reshape(NW, 16, 128).astype(BF)
            st_b[ch] = sy[...].reshape(NW, 16, 128).astype(BF)
        send(st_a, rv_a, ra_sem, 0, g, group)
        if g == 0:
            swap.start()

    send(st_b, rv_b, rb_sem, 1, 0, EXTRA[0])

    make_table(pair_v, table)
    tile = HPAD
    unit = jnp.where(diagonal, 1.0, 0.0).astype(BF)
    for a in range(0, NR, tile):
        b = min(a + tile, NR)
        flipped[:, a:b] = mm(unit, basis[a:b, :], NT).astype(BF)

    save_flip = pltpu.make_async_copy(
        flipped.at[pl.ds(0, LAT), pl.ds(TAIL, NR - TAIL)], flip_out, io_sem.at[6 + len(GROUPS)]
    )
    save_flip.start()

    def couple(first, last):
        for a in range(first * tile, min(last * tile, NR), tile):
            b = min(a + tile, NR)
            factor = 1.0 / (1.0 + rates[...] * spread[0:1, a:b])
            factor = jnp.concatenate([factor, factor], axis=0)
            for r in range(2):
                levels = jnp.concatenate(
                    [state[r, :, a:b], state[2 + r, :, a:b], other[r, :, a:b], other[2 + r, :, a:b]], axis=0
                )
                modes = (mm(down[...], levels, NN) * factor).astype(BF)
                result = mm(up[...], modes, NN).astype(BF)
                state[r, :, a:b] = result[0:64]
                state[2 + r, :, a:b] = result[64:128]

    swap.wait_recv()
    couple(0, 5)

    for g, group in enumerate(FIRST):
        arrive(st_a, rv_a, ra_sem, 0, g, group)
        for ch in range(group[0], sum(group)):
            synthesize(rv_a[ch], table, sx, acc, ch, ch == FIRST[0][0])

    for slot in range(2):
        first, second = slot_terms(acc, slot)
        for f in range(2):
            at = slot * 128 + f * 64
            p, q = first[f].astype(F32), second[f].astype(F32)
            tp[0, at : at + 64, :] = (p + q).astype(BF)
            tp[1, at : at + 64, :] = (p - q).astype(BF)
            store_band(band, slot, f, first[f], second[f], rows_mine > slot + 0.5)
    save_home = pltpu.make_async_copy(band.at[pl.ds(0, 2)], band_out.at[pl.ds(0, 2)], io_sem.at[2])
    save_extra = pltpu.make_async_copy(band.at[pl.ds(2, 2)], band_out.at[pl.ds(2, 2)], io_sem.at[3])
    save_home.start()

    slot_row = iota((2 * NW, LAT), 0)
    weight = [
        jnp.sum(
            jnp.where(slot_row == slot * NW + me, pick[0 : 2 * NW, :].astype(F32) * weights_v[...], 0.0),
            axis=(0, 1), keepdims=True,
        )
        for slot in range(2)
    ]
    for g, group in enumerate(GROUPS):
        for ch in range(group[0], sum(group)):
            for par in range(2):
                coeff = mm(table[par, ch], tp[par], NT).astype(BF).astype(F32)
                for slot in range(2):
                    part = coeff[:, slot * 128 : (slot + 1) * 128] * weight[slot]
                    for r in range(2):
                        for kk in range(2):
                            at = r * 128 + kk * NW
                            sx[pl.ds(kk * 8 + r * 4 + slot * 2 + par, NW, stride=16), :] = part[at : at + NW]
            st_c[ch] = sx[...].reshape(NW, 16, 128).astype(BF)
        send(st_c, rv_c, rc_sem, 2, g, group)

    couple(5, 10)

    arrive(st_b, rv_b, rb_sem, 1, 0, EXTRA[0])
    for ch in range(CHUNKS):
        synthesize(rv_b[ch], table, sx, acc, ch, ch == 0)
    for slot in range(2):
        first, second = slot_terms(acc, slot)
        for f in range(2):
            store_band(band, 2 + slot, f, first[f], second[f], rows_mine > slot + 2.5)
    save_extra.start()

    def forward(g, group):
        at = pl.ds(group[0], group[1])
        return pltpu.make_async_remote_copy(
            src_ref=rv_c.at[at], dst_ref=rv_p.at[at], send_sem=send_sem.at[3, g], recv_sem=rp_sem.at[g],
            device_id={"lev": across}, device_id_type=MESH,
        )

    saves = []

    def save(stop, g):
        a = WINDOWS[2 * GROUPS[g][0]][0]
        at = (pl.ds(0, 4), pl.ds(0, LEVD), pl.ds(a, stop - a))
        copy = pltpu.make_async_copy(state.at[at], new_out.at[at], io_sem.at[4 + g])
        copy.start()
        saves.append(copy)

    def direct(g, group):
        forward(g, group).wait_recv()
        for ch in range(group[0], sum(group)):
            direct_chunk(
                rv_c[ch], rv_p[ch], ch, pair_mine, flipped, 0, spread, rates, pick, down, up, state, sx, sy
            )
        save(WINDOWS[2 * sum(group)][0], g)

    for g, group in enumerate(GROUPS):
        arrive(st_c, rv_c, rc_sem, 2, g, group)
        forward(g, group).start()
        if g > 0:
            direct(g - 1, GROUPS[g - 1])
    save(NR, len(GROUPS) - 1)
    forward(len(GROUPS) - 1, GROUPS[-1]).wait_recv()
    last = pl.ds(LAST, CHUNKS - LAST)
    for i, (ref, out) in enumerate(((rv_c, own_out), (rv_p, across_out))):
        copy = pltpu.make_async_copy(ref.at[last], out, io_sem.at[4 + len(GROUPS) + i])
        copy.start()
        saves.append(copy)
    saves.append(save_flip)

    swap.wait_send()
    for g, group in enumerate(FIRST):
        many(st_a, rv_a, ra_sem, 0, g, group).wait_send()
    for g, group in enumerate(GROUPS):
        many(st_c, rv_c, rc_sem, 2, g, group).wait_send()
        forward(g, group).wait_send()
    many(st_b, rv_b, rb_sem, 1, 0, EXTRA[0]).wait_send()
    save_home.wait()
    save_extra.wait()
    for copy in saves:
        copy.wait()


def local(spectral_state, legendre_basis, pairing, band_rows, weights, mode_rates):
    vmem = pl.BlockSpec(memory_space=pltpu.VMEM)
    anywhere = pl.BlockSpec(memory_space=pl.ANY)
    stage = pltpu.VMEM((CHUNKS, NW, 16, 128), BF)
    work = pltpu.VMEM((NW * 16, 128), F32)
    sems = pltpu.SemaphoreType.DMA((len(GROUPS),))
    results = (
        jax.ShapeDtypeStruct((4, LEVD, NR), BF),
        jax.ShapeDtypeStruct((4, 2, LEVD, NLON), BF),
    )
    part = (CHUNKS - LAST, NW, 16, 128)
    handed = results + (
        jax.ShapeDtypeStruct(part, BF),
        jax.ShapeDtypeStruct(part, BF),
        jax.ShapeDtypeStruct((LAT, NR - TAIL), BF),
    )
    constants = [
        pltpu.VMEM((256, 128), BF),
        pltpu.VMEM((128, 256), BF),
        pltpu.VMEM((256, 256), BF),
        pltpu.VMEM((8, NR), F32),
        pltpu.VMEM((LEV, 1), F32),
    ]
    pairs, rows, rates = pairing.T, band_rows[None, :], mode_rates[None, :]
    passed = pl.pallas_call(
        body,
        out_shape=handed,
        in_specs=[vmem] * 4 + [anywhere] * 2,
        out_specs=(anywhere,) * 5,
        scratch_shapes=[
            pltpu.VMEM((4, LEVD, NR), BF),
            pltpu.VMEM((NR, LAT), BF),
            pltpu.VMEM((LAT, NR), BF),
            pltpu.VMEM((4, 2, LEVD, NLON), BF),
            pltpu.VMEM((4, LEVD, NR), BF),
            pltpu.VMEM((2, CHUNKS, 256, HPAD), BF),
            stage, stage, stage, stage, stage, stage, stage,
            work, work,
            pltpu.VMEM((2, 256, HPAD), F32),
            pltpu.VMEM((2, 256, HPAD), BF),
            *constants,
            pltpu.SemaphoreType.DMA((4, len(GROUPS))),
            sems, sems, sems, sems,
            pltpu.SemaphoreType.DMA((2,)),
            pltpu.SemaphoreType.DMA((3, len(GROUPS))),
            pltpu.SemaphoreType.DMA((7 + len(GROUPS),)),
        ],
        compiler_params=pltpu.CompilerParams(
            collective_id=0, has_side_effects=True, vmem_limit_bytes=VMEM_LIMIT
        ),
    )(pairs, rows, weights[None, :], rates, spectral_state, legendre_basis)
    return pl.pallas_call(
        finish,
        out_shape=results,
        in_specs=[vmem] * 3 + [anywhere] * 5,
        out_specs=(anywhere, anywhere),
        scratch_shapes=[
            pltpu.VMEM((4, LEVD, TAIL), BF),
            pltpu.VMEM((4, LEVD, NR - TAIL), BF),
            pltpu.VMEM((4, 2, LEVD, NLON), BF),
            pltpu.VMEM(part, BF),
            pltpu.VMEM(part, BF),
            pltpu.VMEM((LAT, NR - TAIL), BF),
            work, work,
            *constants,
            pltpu.SemaphoreType.DMA((9,)),
            pltpu.SemaphoreType.DMA((6,)),
        ],
        compiler_params=pltpu.CompilerParams(vmem_limit_bytes=VMEM_LIMIT),
    )(pairs, rows, rates, *passed)


def solution(mesh):
    in_specs = (P(None, "lev", "wave"), P("wave", None), P(), P(), P(), P())
    out_specs = (P(None, "lev", "wave"), P("wave", None, "lev", None))
    return jax.shard_map(local, mesh=mesh, in_specs=in_specs, out_specs=out_specs, check_vma=False)
```

```python
import functools
import math

import jax
import jax.numpy as jnp
from jax import lax
from jax.experimental import pallas as pl
from jax.experimental.pallas import tpu as pltpu
from jax.sharding import PartitionSpec as P

M = 1280
NLON = 2688
HALF = NLON // 2
TILES = 11
HPAD = 128 * TILES
LAT = 128
NW = 64
NR = 12810
LEV = 128
LEVD = 64
ROUNDS = M // (2 * NW)
CHUNKS = ROUNDS // 2
PIECES = []
_offset = 0
for _k in range(ROUNDS):
    _length = 2 * M - 4 * _k * NW - 2 * NW + 1
    PIECES.append((_offset, _length))
    _offset += _length
GROUPS = ((0, 1), (1, 2), (3, 1), (4, 1))
FIRST = ((3, 2), (1, 2), (0, 1))
EXTRA = ((0, CHUNKS),)
LAST = GROUPS[-1][0]
WINDOWS = [(o // 128 * 128, min(-(-(o + n) // 128) * 128, NR)) for o, n in PIECES]
TAIL = WINDOWS[2 * LAST][0]
STEP_WEIGHT = 0.5
VMEM_LIMIT = 61 * 1024 * 1024
BF = jnp.bfloat16
F32 = jnp.float32
I32 = jnp.int32
MESH = pl.DeviceIdType.MESH
NN = (((1,), (0,)), ((), ()))
NT = (((1,), (1,)), ((), ()))
TN = (((0,), (0,)), ((), ()))


def mm(a, b, dims):
    return lax.dot_general(a, b, dims, preferred_element_type=F32)


def iota(shape, dim):
    return lax.broadcasted_iota(I32, shape, dim)


def cos_sin(turns, period):
    rest = turns - jnp.floor(turns * (1.0 / period) + 0.5) * float(period)
    y = rest * (math.pi / period)
    z = y * y
    s = -1.0 / 39916800.0
    for term in (1.0 / 362880.0, -1.0 / 5040.0, 1.0 / 120.0, -1.0 / 6.0, 1.0):
        s = s * z + term
    s = s * y
    c = 1.0 / 479001600.0
    for term in (-1.0 / 3628800.0, 1.0 / 40320.0, -1.0 / 720.0, 1.0 / 24.0, -0.5, 1.0):
        c = c * z + term
    return 1.0 - 2.0 * s * s, 2.0 * s * c


def own_pairs(pair_v, me):
    mine = iota((ROUNDS, NW), 1) == me
    return jnp.sum(jnp.where(mine, pair_v[...], 0).astype(F32), axis=1, keepdims=True).astype(I32)


def rate_column(rates_v):
    diagonal = iota((LEV, LEV), 0) == iota((LEV, LEV), 1)
    return jnp.sum(jnp.where(diagonal, rates_v[...], 0.0), axis=1, keepdims=True)


def round_scalars(pair_mine, k):
    pair = pair_mine[k : k + 1, :]
    begin, length = PIECES[k]
    low = 2 * NW * k + pair
    high = 2 * NW * k + 2 * NW - 1 - pair
    split = begin + M - low
    even = pair % 2 == 0
    end = begin + length
    ranges = (
        jnp.where(even, begin, split),
        jnp.where(even, split, end),
        jnp.where(even, split, begin),
        jnp.where(even, end, split),
    )
    return low, high, split, ranges


def masked_basis(basis, ranges, k):
    a, b = WINDOWS[k]
    rows = a + iota((b - a, 1), 0)
    block = basis[a:b, :].astype(F32)
    even = (rows >= ranges[0]) & (rows < ranges[1])
    odd = (rows >= ranges[2]) & (rows < ranges[3])
    return jnp.concatenate(
        [jnp.where(even, block, 0.0).astype(BF), jnp.where(odd, block, 0.0).astype(BF)], axis=1
    )


def masked_across(flipped, ranges, k, shift):
    a, b = WINDOWS[k]
    rows = a + iota((1, b - a), 1)
    block = flipped[:, a - shift : b - shift].astype(F32)
    even = (rows >= ranges[0]) & (rows < ranges[1])
    odd = (rows >= ranges[2]) & (rows < ranges[3])
    return jnp.concatenate(
        [jnp.where(even, block, 0.0).astype(BF), jnp.where(odd, block, 0.0).astype(BF)], axis=0
    )


def make_picks(rows_v, pick):
    d = iota((NW, NW), 0)
    e = iota((NW, NW), 1)
    count_row = rows_v[...]
    before = e < d
    count = jnp.sum(jnp.where(e == d, count_row, 0).astype(F32), axis=1, keepdims=True)
    starts = jnp.sum(jnp.where(before, count_row, 0).astype(F32), axis=1, keepdims=True)
    single_rank = jnp.sum(jnp.where(before & (count_row == 1), 1.0, 0.0), axis=1, keepdims=True)
    lat = iota((NW, LAT), 1).astype(F32)
    hit = (starts <= lat) & (lat < starts + count)
    slot = jnp.sum(jnp.where(hit, lat - starts, 0.0), axis=0, keepdims=True)
    extra = jnp.where(slot >= 1.5, 1.0, 0.0)
    ahead = jnp.where(iota((LAT, LAT), 0) < iota((LAT, LAT), 1), 1.0, 0.0).astype(BF)
    extra8 = jnp.broadcast_to(extra, (16, LAT)).astype(BF)
    rank = mm(extra8, ahead, NN)[0:1, :]
    adopted = (extra > 0.5) & (rank == single_rank)
    second = jnp.where(count < 1.5, jnp.where(adopted, 1.0, 0.0), jnp.where(lat == starts + 1.0, 1.0, 0.0))
    pick[0:NW, :] = jnp.where(lat == starts, 1.0, 0.0).astype(BF)
    pick[NW : 2 * NW, :] = second.astype(BF)
    pick[2 * NW : 3 * NW, :] = jnp.where(lat == starts + 2.0, 1.0, 0.0).astype(BF)
    pick[3 * NW : 4 * NW, :] = jnp.where(lat == starts + 3.0, 1.0, 0.0).astype(BF)


def make_modes(lev, up, down):
    def fill(mode_index, level_index, same):
        phase = ((2 * level_index + 1) * mode_index).astype(F32)
        cosine, _ = cos_sin(phase, 4 * LEV)
        scale = jnp.where(mode_index == 0, math.sqrt(1.0 / LEV), math.sqrt(2.0 / LEV))
        return jnp.where(same, cosine * scale, 0.0).astype(BF)

    i, j = iota((128, 256), 0), iota((128, 256), 1)
    up[...] = fill(j % LEV, lev * LEVD + i % LEVD, i // LEVD == j // LEV)
    i, j = iota((256, 256), 0), iota((256, 256), 1)
    owner = jnp.where(j < 128, lev, 1 - lev)
    down[...] = fill(i % LEV, owner * LEVD + j % LEVD, i // LEV == (j // LEVD) % 2)


def make_spread(pair_mine, spread, start=0):
    for k in range(start, ROUNDS):
        a, b = WINDOWS[k]
        low, high, split, _ = round_scalars(pair_mine, k)
        rows = a + iota((1, b - a), 1)
        degree = jnp.where(rows < split, rows + (low - PIECES[k][0]), rows + (high - split)).astype(F32)
        value = degree * (degree + 1.0) / float(M * M)
        if k > start:
            width = 128
            first = jnp.where(rows[:, :width] < PIECES[k][0], spread[0:1, a : a + width], value[:, :width])
            spread[0:1, a : a + width] = first
            if b - a > width:
                spread[0:1, a + width : b] = value[:, width:]
        else:
            spread[0:1, a:b] = value


def make_table(pair_v, table):
    lane = iota((128, 128), 1).astype(F32)
    square = iota((NW, NW), 0) == iota((NW, NW), 1)
    for ch in range(CHUNKS):
        pairs = [
            jnp.sum(jnp.where(square, pair_v[k : k + 1, :], 0).astype(F32), axis=1, keepdims=True)
            for k in (2 * ch, 2 * ch + 1)
        ]
        pair = jnp.broadcast_to(jnp.concatenate(pairs, axis=0), (128, 128)).astype(I32)
        base = 2 * NW * (2 * ch + iota((128, 128), 0) // NW)
        low, high = base + pair, base + 2 * NW - 1 - pair
        even = pair % 2 == 0
        for par in range(2):
            wave = (jnp.where(even, low, high) if par == 0 else jnp.where(even, high, low)).astype(F32)
            c, s = cos_sin(wave * lane, NLON)
            c, s = c * NLON ** -0.5, s * NLON ** -0.5
            rc, rs = cos_sin(wave * 128.0, NLON)
            for b in range(TILES):
                lanes = slice(b * 128, (b + 1) * 128)
                if b == TILES - 1:
                    c, s = jnp.where(lane < HALF - 128.0 * b, c, 0.0), jnp.where(lane < HALF - 128.0 * b, s, 0.0)
                table[par, ch, 0:128, lanes] = c.astype(BF)
                table[par, ch, 128:256, lanes] = (-s).astype(BF)
                if b < TILES - 1:
                    c, s = c * rc - s * rs, s * rc + c * rs


def gather_spectra(sx, par):
    return jnp.concatenate(
        [
            jnp.concatenate(
                [
                    sx[pl.ds(kk * 8 + r * 4 + slot * 2 + par, NW, stride=16), :]
                    for r in range(2)
                    for kk in range(2)
                ],
                axis=0,
            )
            for slot in range(2)
        ],
        axis=1,
    ).astype(BF)


def synthesize(land, group, table, sx, acc, first):
    start, count = group
    spectra = [[], []]
    for ch in range(start, start + count):
        sx[...] = land[ch].astype(F32).reshape(NW * 16, 128)
        for par in range(2):
            spectra[par].append(gather_spectra(sx, par))
    for par in range(2):
        waves = table[par, start : start + count].reshape(count * 256, HPAD)
        part = mm(jnp.concatenate(spectra[par], axis=0), waves, TN)
        if first:
            acc[par] = part
        else:
            acc[par] = acc[par] + part


def slot_terms(acc, slot):
    base = slot * 128
    eu, ev = acc[0, base : base + 64, :], acc[0, base + 64 : base + 128, :]
    ou, ov = acc[1, base : base + 64, :], acc[1, base + 64 : base + 128, :]
    out = []
    for u, v in ((eu + ou, ev + ov), (eu - ou, ev - ov)):
        out.append(((-4.0 * u * v).astype(BF), (2.0 * (u * u - v * v)).astype(BF)))
    return out


def store_band(band, slot, f, first, second, keep):
    p = jnp.where(keep, first.astype(F32), 0.0)
    q = jnp.where(keep, second.astype(F32), 0.0)
    rolled = pltpu.roll(q, 64, axis=1)
    band[slot, f, :, 0:1280] = p[:, 0:1280].astype(BF)
    band[slot, f, :, 1280:1408] = (p[:, 1280:1408] + rolled[:, 0:128]).astype(BF)
    band[slot, f, :, 1408:2688] = rolled[:, 128:1408].astype(BF)


def direct_chunk(own, across, ch, pair_mine, flipped, shift, factor_at, pick, down, up, state, sx, sy, between=None):
    sx[...] = own.astype(F32).reshape(NW * 16, 128)
    sy[...] = across.astype(F32).reshape(NW * 16, 128)
    blocks = []
    for kk in range(2):
        for r in range(2):
            for par in range(2):
                at = [kk * 8 + r * 4 + slot * 2 + par for slot in range(2)]
                blocks.append(
                    jnp.concatenate(
                        [jnp.concatenate([s[pl.ds(i, NW, stride=16), :] for i in at], axis=0) for s in (sx, sy)],
                        axis=1,
                    ).astype(BF)
                )
    turned = (mm(down[...], jnp.concatenate(blocks, axis=0), NT) * STEP_WEIGHT).astype(BF)
    tall = jnp.concatenate([turned[:, i * 128 : (i + 1) * 128] for i in range(8)], axis=0)
    placed = mm(tall, pick[0 : 2 * NW, :], NN).astype(BF)
    for kk in range(2):
        if kk == 1 and between is not None:
            between()
        k = 2 * ch + kk
        a, b = WINDOWS[k]
        _, _, _, ranges = round_scalars(pair_mine, k)
        both = masked_across(flipped, ranges, k, shift)
        factor = factor_at(a, b)
        factor = jnp.concatenate([factor, factor], axis=0)
        for r in range(2):
            first = (kk * 2 + r) * 512
            pair = jnp.concatenate([placed[first : first + 256], placed[first + 256 : first + 512]], axis=1)
            modes = (mm(pair, both, NN) * factor).astype(BF)
            change = mm(up[...], modes, NN)
            for f in range(2):
                c = 2 * f + r
                at = slice(a - shift, b - shift)
                state[c, :, at] = (state[c, :, at].astype(F32) + change[f * 64 : (f + 1) * 64]).astype(BF)


def finish(
    pair_v, rows_v, rates_v, new_in, band_in, own_in, across_in, flip_in,
    new_out, band_out,
    state, tail, band, own, across, flipped, sx, sy, pick, up, down, spread, rates, load_sem, save_sem,
):
    me = lax.axis_index("wave")
    lev = lax.axis_index("lev")
    ends = (pl.ds(0, 4), pl.ds(0, LEVD), pl.ds(TAIL, NR - TAIL))
    width = TAIL // 3
    parts = [(pl.ds(0, 4), pl.ds(0, LEVD), pl.ds(i * width, width)) for i in range(3)]
    halves = [pl.ds(0, 2), pl.ds(2, 2)]
    loads = [(new_in.at[at], state.at[at], new_out.at[at]) for at in parts]
    loads += [(band_in.at[at], band.at[at], band_out.at[at]) for at in halves]
    through = [pltpu.make_async_copy(a, b, load_sem.at[i]) for i, (a, b, _) in enumerate(loads)]
    away = [pltpu.make_async_copy(b, c, save_sem.at[i]) for i, (_, b, c) in enumerate(loads)]
    needed = [
        pltpu.make_async_copy(a, b, load_sem.at[len(loads) + i])
        for i, (a, b) in enumerate(
            ((own_in, own), (across_in, across), (flip_in, flipped), (new_in.at[ends], tail))
        )
    ]
    for copy in needed + through:
        copy.start()
    pair_mine = own_pairs(pair_v, me)
    make_picks(rows_v, pick)
    make_modes(lev, up, down)
    make_spread(pair_mine, spread, 2 * LAST)
    rates[...] = rate_column(rates_v)
    def move(first, last):
        for load, save in zip(through[first:last], away[first:last]):
            load.wait()
            save.start()

    for copy in needed:
        copy.wait()
    for ch in range(LAST, CHUNKS):
        direct_chunk(
            own[ch - LAST], across[ch - LAST], ch, pair_mine, flipped, TAIL,
            lambda a, b: 1.0 / (1.0 + rates[...] * spread[0:1, a:b]), pick, down, up, tail, sx, sy,
            functools.partial(move, 0, 2),
        )
    move(2, 5)
    rest = pltpu.make_async_copy(tail, new_out.at[ends], save_sem.at[len(loads)])
    rest.start()
    for copy in away:
        copy.wait()
    rest.wait()


def body(
    pair_v, rows_v, weights_v, rates_v, state_in, basis_in,
    new_out, band_out, own_out, across_out, flip_out,
    state, basis, flipped, band, other, table, st_a, st_b, st_c, rv_a, rv_b, rv_c, rv_p, sx, sy, acc, tp,
    pick, up, down, spread, rates, factors,
    send_sem, ra_sem, rb_sem, rc_sem, rp_sem, state_sem, own_sem, io_sem,
):
    me = lax.axis_index("wave")
    lev = lax.axis_index("lev")
    z, y, x = me // 16, (me // 4) % 4, me % 4
    across = 1 - lev

    load_state = pltpu.make_async_copy(state_in, state, io_sem.at[0])
    load_basis = pltpu.make_async_copy(basis_in, basis, io_sem.at[1])
    load_state.start()
    load_basis.start()

    across_x = [(x + d) % 4 for d in range(4)]

    def each_peer(action):
        def peer(i, d):
            return (z + i // 4 + d + i % 4) % 4 * 16 + (y + i % 4 + d) % 4 * 4 + across_x[d]

        for d in range(1, 4):
            action(peer(0, d))

        def step(i, carry):
            for d in range(4):
                action(peer(i, d))
            return carry

        lax.fori_loop(1, 16, step, 0)

    barrier = pltpu.get_barrier_semaphore()
    each_peer(lambda p: pl.semaphore_signal(barrier, inc=1, device_id={"wave": p}, device_id_type=MESH))
    pl.semaphore_signal(barrier, inc=1, device_id={"lev": across}, device_id_type=MESH)

    pair_mine = own_pairs(pair_v, me)
    make_picks(rows_v, pick)
    make_modes(lev, up, down)
    make_spread(pair_mine, spread)
    diagonal = iota((LEV, LEV), 0) == iota((LEV, LEV), 1)
    rates[...] = rate_column(rates_v)
    rows_mine = jnp.sum(
        jnp.where(iota((1, NW), 1) == me, rows_v[...], 0).astype(F32), axis=1, keepdims=True
    )

    pl.semaphore_wait(barrier, NW)
    swap = pltpu.make_async_remote_copy(
        src_ref=state_in, dst_ref=other, send_sem=state_sem.at[0], recv_sem=state_sem.at[1],
        device_id={"lev": across}, device_id_type=MESH,
    )

    def own(stage, land, which, g, group):
        at = pl.ds(group[0], group[1])
        return pltpu.make_async_copy(stage.at[at, me], land.at[at, me], own_sem.at[which, g])

    def send(stage, land, sems, which, g, group):
        at = pl.ds(group[0], group[1])
        own(stage, land, which, g, group).start()

        def one(p):
            pltpu.make_async_remote_copy(
                src_ref=stage.at[at, p], dst_ref=land.at[at, me], send_sem=send_sem.at[which, g],
                recv_sem=sems.at[g], device_id={"wave": p}, device_id_type=MESH,
            ).start()

        each_peer(one)

    def many(stage, land, sems, which, g, group):
        at = (pl.ds(group[0], group[1]), pl.ds(0, NW - 1))
        return pltpu.make_async_remote_copy(
            src_ref=stage.at[at], dst_ref=land.at[at],
            send_sem=send_sem.at[which, g], recv_sem=sems.at[g], device_id={"wave": me}, device_id_type=MESH,
        )

    def arrive(stage, land, sems, which, g, group):
        own(stage, land, which, g, group).wait()
        many(stage, land, sems, which, g, group).wait_recv()

    load_basis.wait()
    load_state.wait()
    for g, group in enumerate(FIRST):
        for ch in range(group[0], sum(group)):
            for kk in range(2):
                k = 2 * ch + kk
                a, b = WINDOWS[k]
                low, _, _, ranges = round_scalars(pair_mine, k)
                both = masked_basis(basis, ranges, k)
                rows = jnp.concatenate([state[c, :, a:b] for c in (0, 2, 1, 3)], axis=0)
                product = mm(rows, both, NN)
                parts = [product[:, par * LAT : (par + 1) * LAT] for par in range(2)]
                if k == 0:
                    parts[0] = parts[0] * jnp.where(low == 0, 0.5, 1.0)
                picked = mm(pick[...], jnp.concatenate(parts, axis=0).astype(BF), NT)
                for par in range(2):
                    for r in range(2):
                        lanes = slice(par * 256 + r * 128, par * 256 + (r + 1) * 128)
                        for slot in range(2):
                            at = kk * 8 + r * 4 + slot * 2 + par
                            sx[pl.ds(at, NW, stride=16), :] = picked[slot * NW : (slot + 1) * NW, lanes]
                            sy[pl.ds(at, NW, stride=16), :] = picked[(2 + slot) * NW : (3 + slot) * NW, lanes]
            st_a[ch] = sx[...].reshape(NW, 16, 128).astype(BF)
            st_b[ch] = sy[...].reshape(NW, 16, 128).astype(BF)
        send(st_a, rv_a, ra_sem, 0, g, group)
        if g == 0:
            swap.start()

    send(st_b, rv_b, rb_sem, 1, 0, EXTRA[0])

    make_table(pair_v, table)
    tile = HPAD
    unit = jnp.where(diagonal, 1.0, 0.0).astype(BF)
    for a in range(0, NR, tile):
        b = min(a + tile, NR)
        flipped[:, a:b] = mm(unit, basis[a:b, :], NT).astype(BF)

    save_flip = pltpu.make_async_copy(
        flipped.at[pl.ds(0, LAT), pl.ds(TAIL, NR - TAIL)], flip_out, io_sem.at[6 + len(GROUPS)]
    )
    save_flip.start()

    def couple(first, last):
        for a in range(first * tile, min(last * tile, NR), tile):
            b = min(a + tile, NR)
            factor = 1.0 / (1.0 + rates[...] * spread[0:1, a:b])
            factors[:, a:b] = factor
            factor = jnp.concatenate([factor, factor], axis=0)
            for r in range(2):
                levels = jnp.concatenate(
                    [state[r, :, a:b], state[2 + r, :, a:b], other[r, :, a:b], other[2 + r, :, a:b]], axis=0
                )
                modes = (mm(down[...], levels, NN) * factor).astype(BF)
                result = mm(up[...], modes, NN).astype(BF)
                state[r, :, a:b] = result[0:64]
                state[2 + r, :, a:b] = result[64:128]

    swap.wait_recv()
    couple(0, 5)

    for g, group in enumerate(FIRST):
        arrive(st_a, rv_a, ra_sem, 0, g, group)
        synthesize(rv_a, group, table, sx, acc, g == 0)

    for slot in range(2):
        first, second = slot_terms(acc, slot)
        for f in range(2):
            at = slot * 128 + f * 64
            p, q = first[f].astype(F32), second[f].astype(F32)
            tp[0, at : at + 64, :] = (p + q).astype(BF)
            tp[1, at : at + 64, :] = (p - q).astype(BF)
            store_band(band, slot, f, first[f], second[f], rows_mine > slot + 0.5)
    save_home = pltpu.make_async_copy(band.at[pl.ds(0, 2)], band_out.at[pl.ds(0, 2)], io_sem.at[2])
    save_extra = pltpu.make_async_copy(band.at[pl.ds(2, 2)], band_out.at[pl.ds(2, 2)], io_sem.at[3])
    save_home.start()

    slot_row = iota((2 * NW, LAT), 0)
    weight = [
        jnp.sum(
            jnp.where(slot_row == slot * NW + me, pick[0 : 2 * NW, :].astype(F32) * weights_v[...], 0.0),
            axis=(0, 1), keepdims=True,
        )
        for slot in range(2)
    ]
    for g, group in enumerate(GROUPS):
        for ch in range(group[0], sum(group)):
            for par in range(2):
                coeff = mm(table[par, ch], tp[par], NT).astype(BF).astype(F32)
                for slot in range(2):
                    part = coeff[:, slot * 128 : (slot + 1) * 128] * weight[slot]
                    for r in range(2):
                        for kk in range(2):
                            at = r * 128 + kk * NW
                            sx[pl.ds(kk * 8 + r * 4 + slot * 2 + par, NW, stride=16), :] = part[at : at + NW]
            st_c[ch] = sx[...].reshape(NW, 16, 128).astype(BF)
        send(st_c, rv_c, rc_sem, 2, g, group)

    couple(5, 10)

    arrive(st_b, rv_b, rb_sem, 1, 0, EXTRA[0])
    synthesize(rv_b, EXTRA[0], table, sx, acc, True)
    for slot in range(2):
        first, second = slot_terms(acc, slot)
        for f in range(2):
            store_band(band, 2 + slot, f, first[f], second[f], rows_mine > slot + 2.5)
    save_extra.start()

    def forward(g, group):
        at = pl.ds(group[0], group[1])
        return pltpu.make_async_remote_copy(
            src_ref=rv_c.at[at], dst_ref=rv_p.at[at], send_sem=send_sem.at[3, g], recv_sem=rp_sem.at[g],
            device_id={"lev": across}, device_id_type=MESH,
        )

    saves = []

    def save(stop, g):
        a = WINDOWS[2 * GROUPS[g][0]][0]
        at = (pl.ds(0, 4), pl.ds(0, LEVD), pl.ds(a, stop - a))
        copy = pltpu.make_async_copy(state.at[at], new_out.at[at], io_sem.at[4 + g])
        copy.start()
        saves.append(copy)

    def direct(g, group):
        forward(g, group).wait_recv()
        for ch in range(group[0], sum(group)):
            direct_chunk(
                rv_c[ch], rv_p[ch], ch, pair_mine, flipped, 0, lambda a, b: factors[:, a:b],
                pick, down, up, state, sx, sy,
            )
        save(WINDOWS[2 * sum(group)][0], g)

    for g, group in enumerate(GROUPS):
        arrive(st_c, rv_c, rc_sem, 2, g, group)
        forward(g, group).start()
        if g > 0:
            direct(g - 1, GROUPS[g - 1])
    save(NR, len(GROUPS) - 1)
    forward(len(GROUPS) - 1, GROUPS[-1]).wait_recv()
    last = pl.ds(LAST, CHUNKS - LAST)
    for i, (ref, out) in enumerate(((rv_c, own_out), (rv_p, across_out))):
        copy = pltpu.make_async_copy(ref.at[last], out, io_sem.at[4 + len(GROUPS) + i])
        copy.start()
        saves.append(copy)
    saves.append(save_flip)

    swap.wait_send()
    for g, group in enumerate(FIRST):
        many(st_a, rv_a, ra_sem, 0, g, group).wait_send()
    for g, group in enumerate(GROUPS):
        many(st_c, rv_c, rc_sem, 2, g, group).wait_send()
        forward(g, group).wait_send()
    many(st_b, rv_b, rb_sem, 1, 0, EXTRA[0]).wait_send()
    save_home.wait()
    save_extra.wait()
    for copy in saves:
        copy.wait()


def local(spectral_state, legendre_basis, pairing, band_rows, weights, mode_rates):
    vmem = pl.BlockSpec(memory_space=pltpu.VMEM)
    anywhere = pl.BlockSpec(memory_space=pl.ANY)
    stage = pltpu.VMEM((CHUNKS, NW, 16, 128), BF)
    work = pltpu.VMEM((NW * 16, 128), F32)
    sems = pltpu.SemaphoreType.DMA((len(GROUPS),))
    results = (
        jax.ShapeDtypeStruct((4, LEVD, NR), BF),
        jax.ShapeDtypeStruct((4, 2, LEVD, NLON), BF),
    )
    part = (CHUNKS - LAST, NW, 16, 128)
    handed = results + (
        jax.ShapeDtypeStruct(part, BF),
        jax.ShapeDtypeStruct(part, BF),
        jax.ShapeDtypeStruct((LAT, NR - TAIL), BF),
    )
    constants = [
        pltpu.VMEM((256, 128), BF),
        pltpu.VMEM((128, 256), BF),
        pltpu.VMEM((256, 256), BF),
        pltpu.VMEM((8, NR), F32),
        pltpu.VMEM((LEV, 1), F32),
    ]
    pairs, rows, rates = pairing.T, band_rows[None, :], mode_rates[None, :]
    passed = pl.pallas_call(
        body,
        out_shape=handed,
        in_specs=[vmem] * 4 + [anywhere] * 2,
        out_specs=(anywhere,) * 5,
        scratch_shapes=[
            pltpu.VMEM((4, LEVD, NR), BF),
            pltpu.VMEM((NR, LAT), BF),
            pltpu.VMEM((LAT, NR), BF),
            pltpu.VMEM((4, 2, LEVD, NLON), BF),
            pltpu.VMEM((4, LEVD, NR), BF),
            pltpu.VMEM((2, CHUNKS, 256, HPAD), BF),
            stage, stage, stage, stage, stage, stage, stage,
            work, work,
            pltpu.VMEM((2, 256, HPAD), F32),
            pltpu.VMEM((2, 256, HPAD), BF),
            *constants,
            pltpu.VMEM((LEV, NR), F32),
            pltpu.SemaphoreType.DMA((4, len(GROUPS))),
            sems, sems, sems, sems,
            pltpu.SemaphoreType.DMA((2,)),
            pltpu.SemaphoreType.DMA((3, len(GROUPS))),
            pltpu.SemaphoreType.DMA((7 + len(GROUPS),)),
        ],
        compiler_params=pltpu.CompilerParams(
            collective_id=0, has_side_effects=True, vmem_limit_bytes=VMEM_LIMIT
        ),
    )(pairs, rows, weights[None, :], rates, spectral_state, legendre_basis)
    return pl.pallas_call(
        finish,
        out_shape=results,
        in_specs=[vmem] * 3 + [anywhere] * 5,
        out_specs=(anywhere, anywhere),
        scratch_shapes=[
            pltpu.VMEM((4, LEVD, TAIL), BF),
            pltpu.VMEM((4, LEVD, NR - TAIL), BF),
            pltpu.VMEM((4, 2, LEVD, NLON), BF),
            pltpu.VMEM(part, BF),
            pltpu.VMEM(part, BF),
            pltpu.VMEM((LAT, NR - TAIL), BF),
            work, work,
            *constants,
            pltpu.SemaphoreType.DMA((9,)),
            pltpu.SemaphoreType.DMA((6,)),
        ],
        compiler_params=pltpu.CompilerParams(vmem_limit_bytes=VMEM_LIMIT),
    )(pairs, rows, rates, *passed)


def solution(mesh):
    in_specs = (P(None, "lev", "wave"), P("wave", None), P(), P(), P(), P())
    out_specs = (P(None, "lev", "wave"), P("wave", None, "lev", None))
    return jax.shard_map(local, mesh=mesh, in_specs=in_specs, out_specs=out_specs, check_vma=False)
```

```python
import functools
import math

import jax
import jax.numpy as jnp
from jax import lax
from jax.experimental import pallas as pl
from jax.experimental.pallas import tpu as pltpu
from jax.sharding import PartitionSpec as P

M = 1280
NLON = 2688
HALF = NLON // 2
TILES = 11
HPAD = 128 * TILES
LAT = 128
NW = 64
NR = 12810
LEV = 128
LEVD = 64
ROUNDS = M // (2 * NW)
CHUNKS = ROUNDS // 2
PIECES = []
_offset = 0
for _k in range(ROUNDS):
    _length = 2 * M - 4 * _k * NW - 2 * NW + 1
    PIECES.append((_offset, _length))
    _offset += _length
GROUPS = ((0, 1), (1, 2), (3, 1), (4, 1))
FIRST = ((3, 2), (1, 2), (0, 1))
EXTRA = ((0, CHUNKS),)
LAST = GROUPS[-1][0]
WINDOWS = [(o // 128 * 128, min(-(-(o + n) // 128) * 128, NR)) for o, n in PIECES]
TAIL = WINDOWS[2 * LAST][0]
STEP_WEIGHT = 0.5
VMEM_LIMIT = 61 * 1024 * 1024
BF = jnp.bfloat16
F32 = jnp.float32
I32 = jnp.int32
MESH = pl.DeviceIdType.MESH
NN = (((1,), (0,)), ((), ()))
NT = (((1,), (1,)), ((), ()))
TN = (((0,), (0,)), ((), ()))


def mm(a, b, dims):
    return lax.dot_general(a, b, dims, preferred_element_type=F32)


def iota(shape, dim):
    return lax.broadcasted_iota(I32, shape, dim)


def cos_sin(turns, period):
    rest = turns - jnp.floor(turns * (1.0 / period) + 0.5) * float(period)
    y = rest * (math.pi / period)
    z = y * y
    s = -1.0 / 39916800.0
    for term in (1.0 / 362880.0, -1.0 / 5040.0, 1.0 / 120.0, -1.0 / 6.0, 1.0):
        s = s * z + term
    s = s * y
    c = 1.0 / 479001600.0
    for term in (-1.0 / 3628800.0, 1.0 / 40320.0, -1.0 / 720.0, 1.0 / 24.0, -0.5, 1.0):
        c = c * z + term
    return 1.0 - 2.0 * s * s, 2.0 * s * c


def own_pairs(pair_v, me):
    mine = iota((ROUNDS, NW), 1) == me
    return jnp.sum(jnp.where(mine, pair_v[...], 0).astype(F32), axis=1, keepdims=True).astype(I32)


def rate_column(rates_v):
    diagonal = iota((LEV, LEV), 0) == iota((LEV, LEV), 1)
    return jnp.sum(jnp.where(diagonal, rates_v[...], 0.0), axis=1, keepdims=True)


def round_scalars(pair_mine, k):
    pair = pair_mine[k : k + 1, :]
    begin, length = PIECES[k]
    low = 2 * NW * k + pair
    high = 2 * NW * k + 2 * NW - 1 - pair
    split = begin + M - low
    even = pair % 2 == 0
    end = begin + length
    ranges = (
        jnp.where(even, begin, split),
        jnp.where(even, split, end),
        jnp.where(even, split, begin),
        jnp.where(even, end, split),
    )
    return low, high, split, ranges


def masked_basis(basis, ranges, k):
    a, b = WINDOWS[k]
    rows = a + iota((b - a, 1), 0)
    block = basis[a:b, :].astype(F32)
    even = (rows >= ranges[0]) & (rows < ranges[1])
    odd = (rows >= ranges[2]) & (rows < ranges[3])
    return jnp.concatenate(
        [jnp.where(even, block, 0.0).astype(BF), jnp.where(odd, block, 0.0).astype(BF)], axis=1
    )


def masked_across(flipped, ranges, k, shift):
    a, b = WINDOWS[k]
    rows = a + iota((1, b - a), 1)
    block = flipped[:, a - shift : b - shift].astype(F32)
    even = (rows >= ranges[0]) & (rows < ranges[1])
    odd = (rows >= ranges[2]) & (rows < ranges[3])
    return jnp.concatenate(
        [jnp.where(even, block, 0.0).astype(BF), jnp.where(odd, block, 0.0).astype(BF)], axis=0
    )


def make_picks(rows_v, pick):
    d = iota((NW, NW), 0)
    e = iota((NW, NW), 1)
    count_row = rows_v[...]
    before = e < d
    count = jnp.sum(jnp.where(e == d, count_row, 0).astype(F32), axis=1, keepdims=True)
    starts = jnp.sum(jnp.where(before, count_row, 0).astype(F32), axis=1, keepdims=True)
    single_rank = jnp.sum(jnp.where(before & (count_row == 1), 1.0, 0.0), axis=1, keepdims=True)
    lat = iota((NW, LAT), 1).astype(F32)
    hit = (starts <= lat) & (lat < starts + count)
    slot = jnp.sum(jnp.where(hit, lat - starts, 0.0), axis=0, keepdims=True)
    extra = jnp.where(slot >= 1.5, 1.0, 0.0)
    ahead = jnp.where(iota((LAT, LAT), 0) < iota((LAT, LAT), 1), 1.0, 0.0).astype(BF)
    extra8 = jnp.broadcast_to(extra, (16, LAT)).astype(BF)
    rank = mm(extra8, ahead, NN)[0:1, :]
    adopted = (extra > 0.5) & (rank == single_rank)
    second = jnp.where(count < 1.5, jnp.where(adopted, 1.0, 0.0), jnp.where(lat == starts + 1.0, 1.0, 0.0))
    pick[0:NW, :] = jnp.where(lat == starts, 1.0, 0.0).astype(BF)
    pick[NW : 2 * NW, :] = second.astype(BF)
    pick[2 * NW : 3 * NW, :] = jnp.where(lat == starts + 2.0, 1.0, 0.0).astype(BF)
    pick[3 * NW : 4 * NW, :] = jnp.where(lat == starts + 3.0, 1.0, 0.0).astype(BF)


def make_modes(lev, up, down):
    def fill(mode_index, level_index, same):
        phase = ((2 * level_index + 1) * mode_index).astype(F32)
        cosine, _ = cos_sin(phase, 4 * LEV)
        scale = jnp.where(mode_index == 0, math.sqrt(1.0 / LEV), math.sqrt(2.0 / LEV))
        return jnp.where(same, cosine * scale, 0.0).astype(BF)

    i, j = iota((128, 256), 0), iota((128, 256), 1)
    up[...] = fill(j % LEV, lev * LEVD + i % LEVD, i // LEVD == j // LEV)
    i, j = iota((256, 256), 0), iota((256, 256), 1)
    owner = jnp.where(j < 128, lev, 1 - lev)
    down[...] = fill(i % LEV, owner * LEVD + j % LEVD, i // LEV == (j // LEVD) % 2)


def make_spread(pair_mine, spread, start=0):
    for k in range(start, ROUNDS):
        a, b = WINDOWS[k]
        low, high, split, _ = round_scalars(pair_mine, k)
        rows = a + iota((1, b - a), 1)
        degree = jnp.where(rows < split, rows + (low - PIECES[k][0]), rows + (high - split)).astype(F32)
        value = degree * (degree + 1.0) / float(M * M)
        if k > start:
            width = 128
            first = jnp.where(rows[:, :width] < PIECES[k][0], spread[0:1, a : a + width], value[:, :width])
            spread[0:1, a : a + width] = first
            if b - a > width:
                spread[0:1, a + width : b] = value[:, width:]
        else:
            spread[0:1, a:b] = value


def make_table(pair_v, table):
    lane = iota((128, 128), 1).astype(F32)
    square = iota((NW, NW), 0) == iota((NW, NW), 1)
    for ch in range(CHUNKS):
        pairs = [
            jnp.sum(jnp.where(square, pair_v[k : k + 1, :], 0).astype(F32), axis=1, keepdims=True)
            for k in (2 * ch, 2 * ch + 1)
        ]
        pair = jnp.broadcast_to(jnp.concatenate(pairs, axis=0), (128, 128)).astype(I32)
        base = 2 * NW * (2 * ch + iota((128, 128), 0) // NW)
        low, high = base + pair, base + 2 * NW - 1 - pair
        even = pair % 2 == 0
        for par in range(2):
            wave = (jnp.where(even, low, high) if par == 0 else jnp.where(even, high, low)).astype(F32)
            c, s = cos_sin(wave * lane, NLON)
            c, s = c * NLON ** -0.5, s * NLON ** -0.5
            rc, rs = cos_sin(wave * 128.0, NLON)
            for b in range(TILES):
                lanes = slice(b * 128, (b + 1) * 128)
                if b == TILES - 1:
                    c, s = jnp.where(lane < HALF - 128.0 * b, c, 0.0), jnp.where(lane < HALF - 128.0 * b, s, 0.0)
                table[par, ch, 0:128, lanes] = c.astype(BF)
                table[par, ch, 128:256, lanes] = (-s).astype(BF)
                if b < TILES - 1:
                    c, s = c * rc - s * rs, s * rc + c * rs


def gather_spectra(sx, par):
    return jnp.concatenate(
        [
            jnp.concatenate(
                [
                    sx[pl.ds(kk * 8 + r * 4 + slot * 2 + par, NW, stride=16), :]
                    for r in range(2)
                    for kk in range(2)
                ],
                axis=0,
            )
            for slot in range(2)
        ],
        axis=1,
    ).astype(BF)


def synthesize(x, table, sx, acc, ch, first):
    sx[...] = x.astype(F32).reshape(NW * 16, 128)
    for par in range(2):
        part = mm(gather_spectra(sx, par), table[par, ch], TN)
        if first:
            acc[par] = part
        else:
            acc[par] = acc[par] + part


def slot_terms(acc, slot):
    base = slot * 128
    eu, ev = acc[0, base : base + 64, :], acc[0, base + 64 : base + 128, :]
    ou, ov = acc[1, base : base + 64, :], acc[1, base + 64 : base + 128, :]
    out = []
    for u, v in ((eu + ou, ev + ov), (eu - ou, ev - ov)):
        out.append(((-4.0 * u * v).astype(BF), (2.0 * (u * u - v * v)).astype(BF)))
    return out


def store_band(band, slot, f, first, second, keep):
    p = jnp.where(keep, first.astype(F32), 0.0)
    q = jnp.where(keep, second.astype(F32), 0.0)
    rolled = pltpu.roll(q, 64, axis=1)
    band[slot, f, :, 0:1280] = p[:, 0:1280].astype(BF)
    band[slot, f, :, 1280:1408] = (p[:, 1280:1408] + rolled[:, 0:128]).astype(BF)
    band[slot, f, :, 1408:2688] = rolled[:, 128:1408].astype(BF)


def direct_chunk(own, across, ch, pair_mine, flipped, shift, factor_at, pick, down, up, state, sx, sy, between=None):
    sx[...] = own.astype(F32).reshape(NW * 16, 128)
    sy[...] = across.astype(F32).reshape(NW * 16, 128)
    blocks = []
    for kk in range(2):
        for r in range(2):
            for par in range(2):
                at = [kk * 8 + r * 4 + slot * 2 + par for slot in range(2)]
                blocks.append(
                    jnp.concatenate(
                        [jnp.concatenate([s[pl.ds(i, NW, stride=16), :] for i in at], axis=0) for s in (sx, sy)],
                        axis=1,
                    ).astype(BF)
                )
    turned = (mm(down[...], jnp.concatenate(blocks, axis=0), NT) * STEP_WEIGHT).astype(BF)
    tall = jnp.concatenate([turned[:, i * 128 : (i + 1) * 128] for i in range(8)], axis=0)
    placed = mm(tall, pick[0 : 2 * NW, :], NN).astype(BF)
    for kk in range(2):
        if kk == 1 and between is not None:
            between()
        k = 2 * ch + kk
        a, b = WINDOWS[k]
        _, _, _, ranges = round_scalars(pair_mine, k)
        both = masked_across(flipped, ranges, k, shift)
        factor = factor_at(a, b)
        factor = jnp.concatenate([factor, factor], axis=0)
        for r in range(2):
            first = (kk * 2 + r) * 512
            pair = jnp.concatenate([placed[first : first + 256], placed[first + 256 : first + 512]], axis=1)
            modes = (mm(pair, both, NN) * factor).astype(BF)
            change = mm(up[...], modes, NN)
            for f in range(2):
                c = 2 * f + r
                at = slice(a - shift, b - shift)
                state[c, :, at] = (state[c, :, at].astype(F32) + change[f * 64 : (f + 1) * 64]).astype(BF)


def finish(
    pair_v, rows_v, rates_v, new_in, band_in, own_in, across_in, flip_in,
    new_out, band_out,
    state, tail, band, own, across, flipped, sx, sy, pick, up, down, spread, rates, load_sem, save_sem,
):
    me = lax.axis_index("wave")
    lev = lax.axis_index("lev")
    ends = (pl.ds(0, 4), pl.ds(0, LEVD), pl.ds(TAIL, NR - TAIL))
    width = TAIL // 3
    parts = [(pl.ds(0, 4), pl.ds(0, LEVD), pl.ds(i * width, width)) for i in range(3)]
    halves = [pl.ds(0, 2), pl.ds(2, 2)]
    loads = [(new_in.at[at], state.at[at], new_out.at[at]) for at in parts]
    loads += [(band_in.at[at], band.at[at], band_out.at[at]) for at in halves]
    through = [pltpu.make_async_copy(a, b, load_sem.at[i]) for i, (a, b, _) in enumerate(loads)]
    away = [pltpu.make_async_copy(b, c, save_sem.at[i]) for i, (_, b, c) in enumerate(loads)]
    needed = [
        pltpu.make_async_copy(a, b, load_sem.at[len(loads) + i])
        for i, (a, b) in enumerate(
            ((own_in, own), (across_in, across), (flip_in, flipped), (new_in.at[ends], tail))
        )
    ]
    for copy in needed + through:
        copy.start()
    pair_mine = own_pairs(pair_v, me)
    make_picks(rows_v, pick)
    make_modes(lev, up, down)
    make_spread(pair_mine, spread, 2 * LAST)
    rates[...] = rate_column(rates_v)
    def move(first, last):
        for load, save in zip(through[first:last], away[first:last]):
            load.wait()
            save.start()

    for copy in needed:
        copy.wait()
    for ch in range(LAST, CHUNKS):
        direct_chunk(
            own[ch - LAST], across[ch - LAST], ch, pair_mine, flipped, TAIL,
            lambda a, b: 1.0 / (1.0 + rates[...] * spread[0:1, a:b]), pick, down, up, tail, sx, sy,
            functools.partial(move, 0, 2),
        )
    move(2, 5)
    rest = pltpu.make_async_copy(tail, new_out.at[ends], save_sem.at[len(loads)])
    rest.start()
    for copy in away:
        copy.wait()
    rest.wait()


def body(
    pair_v, rows_v, weights_v, rates_v, state_in, basis_in,
    new_out, band_out, own_out, across_out, flip_out,
    state, basis, flipped, band, other, table, st_a, st_b, st_c, rv_a, rv_b, rv_c, rv_p, sx, sy, acc, tp,
    pick, up, down, spread, rates,
    send_sem, ra_sem, rb_sem, rc_sem, rp_sem, state_sem, own_sem, io_sem,
):
    me = lax.axis_index("wave")
    lev = lax.axis_index("lev")
    z, y, x = me // 16, (me // 4) % 4, me % 4
    across = 1 - lev

    load_state = pltpu.make_async_copy(state_in, state, io_sem.at[0])
    load_basis = pltpu.make_async_copy(basis_in, basis, io_sem.at[1])
    load_state.start()
    load_basis.start()

    across_x = [(x + d) % 4 for d in range(4)]

    def each_peer(action):
        def peer(i, d):
            return (z + i // 4 + d + i % 4) % 4 * 16 + (y + i % 4 + d) % 4 * 4 + across_x[d]

        for d in range(1, 4):
            action(peer(0, d))

        def step(i, carry):
            for d in range(4):
                action(peer(i, d))
            return carry

        lax.fori_loop(1, 16, step, 0)

    barrier = pltpu.get_barrier_semaphore()
    each_peer(lambda p: pl.semaphore_signal(barrier, inc=1, device_id={"wave": p}, device_id_type=MESH))
    pl.semaphore_signal(barrier, inc=1, device_id={"lev": across}, device_id_type=MESH)

    pair_mine = own_pairs(pair_v, me)
    make_picks(rows_v, pick)
    make_modes(lev, up, down)
    make_spread(pair_mine, spread)
    diagonal = iota((LEV, LEV), 0) == iota((LEV, LEV), 1)
    rates[...] = rate_column(rates_v)
    rows_mine = jnp.sum(
        jnp.where(iota((1, NW), 1) == me, rows_v[...], 0).astype(F32), axis=1, keepdims=True
    )

    pl.semaphore_wait(barrier, NW)
    swap = pltpu.make_async_remote_copy(
        src_ref=state_in, dst_ref=other, send_sem=state_sem.at[0], recv_sem=state_sem.at[1],
        device_id={"lev": across}, device_id_type=MESH,
    )

    def own(stage, land, which, g, group):
        at = pl.ds(group[0], group[1])
        return pltpu.make_async_copy(stage.at[at, me], land.at[at, me], own_sem.at[which, g])

    def send(stage, land, sems, which, g, group):
        at = pl.ds(group[0], group[1])
        own(stage, land, which, g, group).start()

        def one(p):
            pltpu.make_async_remote_copy(
                src_ref=stage.at[at, p], dst_ref=land.at[at, me], send_sem=send_sem.at[which, g],
                recv_sem=sems.at[g], device_id={"wave": p}, device_id_type=MESH,
            ).start()

        each_peer(one)

    def many(stage, land, sems, which, g, group):
        at = (pl.ds(group[0], group[1]), pl.ds(0, NW - 1))
        return pltpu.make_async_remote_copy(
            src_ref=stage.at[at], dst_ref=land.at[at],
            send_sem=send_sem.at[which, g], recv_sem=sems.at[g], device_id={"wave": me}, device_id_type=MESH,
        )

    def arrive(stage, land, sems, which, g, group):
        own(stage, land, which, g, group).wait()
        many(stage, land, sems, which, g, group).wait_recv()

    load_basis.wait()
    load_state.wait()
    for g, group in enumerate(FIRST):
        for ch in range(group[0], sum(group)):
            for kk in range(2):
                k = 2 * ch + kk
                a, b = WINDOWS[k]
                low, _, _, ranges = round_scalars(pair_mine, k)
                both = masked_basis(basis, ranges, k)
                rows = jnp.concatenate([state[c, :, a:b] for c in (0, 2, 1, 3)], axis=0)
                product = mm(rows, both, NN)
                for par in range(2):
                    part = product[:, par * LAT : (par + 1) * LAT]
                    if k == 0 and par == 0:
                        part = part * jnp.where(low == 0, 0.5, 1.0)
                    picked = mm(pick[...], part.astype(BF), NT)
                    for r in range(2):
                        lanes = slice(r * 128, (r + 1) * 128)
                        for slot in range(2):
                            at = kk * 8 + r * 4 + slot * 2 + par
                            sx[pl.ds(at, NW, stride=16), :] = picked[slot * NW : (slot + 1) * NW, lanes]
                            sy[pl.ds(at, NW, stride=16), :] = picked[(2 + slot) * NW : (3 + slot) * NW, lanes]
            st_a[ch] = sx[...].reshape(NW, 16, 128).astype(BF)
            st_b[ch] = sy[...].reshape(NW, 16, 128).astype(BF)
        send(st_a, rv_a, ra_sem, 0, g, group)
        if g == 0:
            swap.start()

    send(st_b, rv_b, rb_sem, 1, 0, EXTRA[0])

    make_table(pair_v, table)
    tile = HPAD
    unit = jnp.where(diagonal, 1.0, 0.0).astype(BF)
    for a in range(0, NR, tile):
        b = min(a + tile, NR)
        flipped[:, a:b] = mm(unit, basis[a:b, :], NT).astype(BF)

    save_flip = pltpu.make_async_copy(
        flipped.at[pl.ds(0, LAT), pl.ds(TAIL, NR - TAIL)], flip_out, io_sem.at[6 + len(GROUPS)]
    )
    save_flip.start()

    def couple(first, last):
        for a in range(first * tile, min(last * tile, NR), tile):
            b = min(a + tile, NR)
            factor = 1.0 / (1.0 + rates[...] * spread[0:1, a:b])
            factor = jnp.concatenate([factor, factor], axis=0)
            for r in range(2):
                levels = jnp.concatenate(
                    [state[r, :, a:b], state[2 + r, :, a:b], other[r, :, a:b], other[2 + r, :, a:b]], axis=0
                )
                modes = (mm(down[...], levels, NN) * factor).astype(BF)
                result = mm(up[...], modes, NN).astype(BF)
                state[r, :, a:b] = result[0:64]
                state[2 + r, :, a:b] = result[64:128]

    swap.wait_recv()
    couple(0, 5)

    for g, group in enumerate(FIRST):
        arrive(st_a, rv_a, ra_sem, 0, g, group)
        for ch in range(group[0], sum(group)):
            synthesize(rv_a[ch], table, sx, acc, ch, ch == FIRST[0][0])

    for slot in range(2):
        first, second = slot_terms(acc, slot)
        for f in range(2):
            at = slot * 128 + f * 64
            p, q = first[f].astype(F32), second[f].astype(F32)
            tp[0, at : at + 64, :] = (p + q).astype(BF)
            tp[1, at : at + 64, :] = (p - q).astype(BF)
            store_band(band, slot, f, first[f], second[f], rows_mine > slot + 0.5)
    save_home = pltpu.make_async_copy(band.at[pl.ds(0, 2)], band_out.at[pl.ds(0, 2)], io_sem.at[2])
    save_extra = pltpu.make_async_copy(band.at[pl.ds(2, 2)], band_out.at[pl.ds(2, 2)], io_sem.at[3])
    save_home.start()

    slot_row = iota((2 * NW, LAT), 0)
    weight = [
        jnp.sum(
            jnp.where(slot_row == slot * NW + me, pick[0 : 2 * NW, :].astype(F32) * weights_v[...], 0.0),
            axis=(0, 1), keepdims=True,
        )
        for slot in range(2)
    ]
    for g, group in enumerate(GROUPS):
        for ch in range(group[0], sum(group)):
            for par in range(2):
                coeff = mm(table[par, ch], tp[par], NT).astype(BF).astype(F32)
                for slot in range(2):
                    part = coeff[:, slot * 128 : (slot + 1) * 128] * weight[slot]
                    for r in range(2):
                        for kk in range(2):
                            at = r * 128 + kk * NW
                            sx[pl.ds(kk * 8 + r * 4 + slot * 2 + par, NW, stride=16), :] = part[at : at + NW]
            st_c[ch] = sx[...].reshape(NW, 16, 128).astype(BF)
        send(st_c, rv_c, rc_sem, 2, g, group)

    couple(5, 10)

    arrive(st_b, rv_b, rb_sem, 1, 0, EXTRA[0])
    for ch in range(CHUNKS):
        synthesize(rv_b[ch], table, sx, acc, ch, ch == 0)
    for slot in range(2):
        first, second = slot_terms(acc, slot)
        for f in range(2):
            store_band(band, 2 + slot, f, first[f], second[f], rows_mine > slot + 2.5)
    save_extra.start()

    def forward(g, group):
        at = pl.ds(group[0], group[1])
        return pltpu.make_async_remote_copy(
            src_ref=rv_c.at[at], dst_ref=rv_p.at[at], send_sem=send_sem.at[3, g], recv_sem=rp_sem.at[g],
            device_id={"lev": across}, device_id_type=MESH,
        )

    saves = []

    def save(stop, g):
        a = WINDOWS[2 * GROUPS[g][0]][0]
        at = (pl.ds(0, 4), pl.ds(0, LEVD), pl.ds(a, stop - a))
        copy = pltpu.make_async_copy(state.at[at], new_out.at[at], io_sem.at[4 + g])
        copy.start()
        saves.append(copy)

    def direct(g, group):
        forward(g, group).wait_recv()
        for ch in range(group[0], sum(group)):
            direct_chunk(
                rv_c[ch], rv_p[ch], ch, pair_mine, flipped, 0, lambda a, b: 1.0 / (1.0 + rates[...] * spread[0:1, a:b]),
                pick, down, up, state, sx, sy,
            )
        save(WINDOWS[2 * sum(group)][0], g)

    for g, group in enumerate(GROUPS):
        arrive(st_c, rv_c, rc_sem, 2, g, group)
        forward(g, group).start()
        if g > 0:
            direct(g - 1, GROUPS[g - 1])
    save(NR, len(GROUPS) - 1)
    forward(len(GROUPS) - 1, GROUPS[-1]).wait_recv()
    last = pl.ds(LAST, CHUNKS - LAST)
    for i, (ref, out) in enumerate(((rv_c, own_out), (rv_p, across_out))):
        copy = pltpu.make_async_copy(ref.at[last], out, io_sem.at[4 + len(GROUPS) + i])
        copy.start()
        saves.append(copy)
    saves.append(save_flip)

    swap.wait_send()
    for g, group in enumerate(FIRST):
        many(st_a, rv_a, ra_sem, 0, g, group).wait_send()
    for g, group in enumerate(GROUPS):
        many(st_c, rv_c, rc_sem, 2, g, group).wait_send()
        forward(g, group).wait_send()
    many(st_b, rv_b, rb_sem, 1, 0, EXTRA[0]).wait_send()
    save_home.wait()
    save_extra.wait()
    for copy in saves:
        copy.wait()


def local(spectral_state, legendre_basis, pairing, band_rows, weights, mode_rates):
    vmem = pl.BlockSpec(memory_space=pltpu.VMEM)
    anywhere = pl.BlockSpec(memory_space=pl.ANY)
    stage = pltpu.VMEM((CHUNKS, NW, 16, 128), BF)
    work = pltpu.VMEM((NW * 16, 128), F32)
    sems = pltpu.SemaphoreType.DMA((len(GROUPS),))
    results = (
        jax.ShapeDtypeStruct((4, LEVD, NR), BF),
        jax.ShapeDtypeStruct((4, 2, LEVD, NLON), BF),
    )
    part = (CHUNKS - LAST, NW, 16, 128)
    handed = results + (
        jax.ShapeDtypeStruct(part, BF),
        jax.ShapeDtypeStruct(part, BF),
        jax.ShapeDtypeStruct((LAT, NR - TAIL), BF),
    )
    constants = [
        pltpu.VMEM((256, 128), BF),
        pltpu.VMEM((128, 256), BF),
        pltpu.VMEM((256, 256), BF),
        pltpu.VMEM((8, NR), F32),
        pltpu.VMEM((LEV, 1), F32),
    ]
    pairs, rows, rates = pairing.T, band_rows[None, :], mode_rates[None, :]
    passed = pl.pallas_call(
        body,
        out_shape=handed,
        in_specs=[vmem] * 4 + [anywhere] * 2,
        out_specs=(anywhere,) * 5,
        scratch_shapes=[
            pltpu.VMEM((4, LEVD, NR), BF),
            pltpu.VMEM((NR, LAT), BF),
            pltpu.VMEM((LAT, NR), BF),
            pltpu.VMEM((4, 2, LEVD, NLON), BF),
            pltpu.VMEM((4, LEVD, NR), BF),
            pltpu.VMEM((2, CHUNKS, 256, HPAD), BF),
            stage, stage, stage, stage, stage, stage, stage,
            work, work,
            pltpu.VMEM((2, 256, HPAD), F32),
            pltpu.VMEM((2, 256, HPAD), BF),
            *constants,
            pltpu.SemaphoreType.DMA((4, len(GROUPS))),
            sems, sems, sems, sems,
            pltpu.SemaphoreType.DMA((2,)),
            pltpu.SemaphoreType.DMA((3, len(GROUPS))),
            pltpu.SemaphoreType.DMA((7 + len(GROUPS),)),
        ],
        compiler_params=pltpu.CompilerParams(
            collective_id=0, has_side_effects=True, vmem_limit_bytes=VMEM_LIMIT
        ),
    )(pairs, rows, weights[None, :], rates, spectral_state, legendre_basis)
    return pl.pallas_call(
        finish,
        out_shape=results,
        in_specs=[vmem] * 3 + [anywhere] * 5,
        out_specs=(anywhere, anywhere),
        scratch_shapes=[
            pltpu.VMEM((4, LEVD, TAIL), BF),
            pltpu.VMEM((4, LEVD, NR - TAIL), BF),
            pltpu.VMEM((4, 2, LEVD, NLON), BF),
            pltpu.VMEM(part, BF),
            pltpu.VMEM(part, BF),
            pltpu.VMEM((LAT, NR - TAIL), BF),
            work, work,
            *constants,
            pltpu.SemaphoreType.DMA((9,)),
            pltpu.SemaphoreType.DMA((6,)),
        ],
        compiler_params=pltpu.CompilerParams(vmem_limit_bytes=VMEM_LIMIT),
    )(pairs, rows, rates, *passed)


def solution(mesh):
    in_specs = (P(None, "lev", "wave"), P("wave", None), P(), P(), P(), P())
    out_specs = (P(None, "lev", "wave"), P("wave", None, "lev", None))
    return jax.shard_map(local, mesh=mesh, in_specs=in_specs, out_specs=out_specs, check_vma=False)
```
